32 devices in a mesh: span: 16 (over z, y, x), width: 2 (over core).
Axes of the slice: x: 2, y: 2, z: 4, core: 2. Of those that a mesh axis runs over, the one named last changes fastest.
Arguments:
- state: float32 [4, 128, 64, 128], P(None, 'span', 'width'), may hold values from 0.2 to 2
- source: float32 [4, 128, 64, 128], P(None, 'span', 'width'), may hold values from -6 to 8
- conductance: float32 [128, 64, 128], P('span', 'width'), may hold values from 0.5 to 2
- rebar_cover: int32 [128, 64, 128], P('span', 'width'), may hold values 0 or 1
- colour: int32 [16, 2], P('span', 'width'), may hold values from 0 to 1
- diffusivity: float32 [4], replicated, may hold values from 0.5 to 2
- binding: float32 [4], replicated, may hold values from 0.1 to 1
Outputs:
- updated: float32 [4, 128, 64, 128], P(None, 'span', 'width')
- residual: float32 [4, 128, 64, 128], P(None, 'span', 'width')
The draws below stay inside these ranges and needn't reach their ends.
All inputs are finite; a program needn't handle non-finite values. No bound on the sum of `rebar_cover` on one device may be relied on, other than what follows from the above.
Results may differ from the reference program's by a relative error of at most 0.002.
Values sent between devices are 32-bit elements; how exact they have to be, the bound alone decides.
A program may use at most 64 MiB of HBM per device.

```python
import math
import jax
import jax.numpy as jnp
from jax import lax

IONS = 4
COARSEN = 8
SWEEPS = 4
COARSE_ITERS = 20
CX = 8
CY = 32
NX = 128
NY = 64
NZ = 128
N_SPAN = 16
N_WIDTH = 2


def draw_source(key, part):
    key_noise = jax.random.fold_in(key, 11)
    key_amp = jax.random.fold_in(key, 12)
    key_phase = jax.random.fold_in(key, 13)
    xs = jnp.arange(NX, dtype=jnp.float32)[None, :, None, None] / NX
    zs = jnp.arange(NZ, dtype=jnp.float32)[None, None, None, :] / NZ
    phase = jax.random.uniform(key_phase, (IONS, 1, 1, 1), jnp.float32, 0.0, 6.2831853)
    profile = 1.0 + 0.5 * jnp.sin(6.2831853 * xs + phase) * jnp.cos(3.1415927 * zs)
    amp = jax.random.uniform(key_amp, (IONS, 1, 1, 1), jnp.float32, 0.6, 1.4)
    noise = jax.random.normal(key_noise, (IONS, NX, NY, NZ), jnp.float32)
    return jnp.clip(amp * profile + noise, -6.0, 8.0)


def set_ends(entries, own_key, smallest, top_value):
    shape = entries.shape
    index_at = [jax.random.randint(jax.random.fold_in(own_key, axis), (), 0, shape[axis]) for axis in range(len(shape))]
    entries = entries.at[tuple(index_at)].set(smallest)
    longest = shape.index(max(shape))
    index_at[longest] = (index_at[longest] + 1) % shape[longest]
    return entries.at[tuple(index_at)].set(top_value)


def level_of(stream_key, extent, pieces, least, largest):
    factor_of, own = 1.0, jax.random.fold_in(stream_key, 6)
    for axis_at, blocks in pieces:
        steps = jnp.exp(jax.random.uniform(jax.random.fold_in(own, axis_at), (blocks,), jnp.float32, least / len(pieces), largest / len(pieces)))
        factor_of = factor_of * jnp.repeat(steps, extent[axis_at] // blocks).reshape([-1 if axis == axis_at else 1 for axis in range(len(extent))])
    return factor_of


def setup_inputs(seed: int = 0) -> dict:
    arg_keys = jax.random.split(jax.random.key(seed), 8)
    return {
        "state": jnp.clip(0.2 + 1.8 * jax.random.uniform(arg_keys[0], (IONS, NX, NY, NZ), jnp.float32) ** level_of(arg_keys[0], (IONS, NX, NY, NZ), ((1, 16), (2, 2)), -0.2, 0.2), 0.2, 2.0),
        "source": draw_source(jax.random.fold_in(arg_keys[7], 71), 0),
        "conductance": jnp.clip(jnp.exp(math.log(2.0) - 1.3862944 * jax.random.uniform(arg_keys[2], (NX, NY, NZ), jnp.float32) ** level_of(arg_keys[2], (NX, NY, NZ), ((0, 16), (1, 2)), -0.2, 0.2)), 0.5, 2.0),
        "rebar_cover": set_ends((jax.random.randint(arg_keys[3], (NX, NY, NZ), 0, 2) < 1).astype(jnp.int32), jax.random.fold_in(arg_keys[3], 1), 0, 1),
        "colour": set_ends(jax.random.randint(arg_keys[4], (N_SPAN, N_WIDTH), 0, 2), jax.random.fold_in(arg_keys[4], 1), 0, 1).astype(jnp.int32),
        "diffusivity": jnp.clip(jnp.exp(jax.random.uniform(arg_keys[5], (IONS,), jnp.float32, math.log(0.5), math.log(2.0))), 0.5, 2.0),
        "binding": jnp.clip(jnp.exp(jax.random.uniform(arg_keys[6], (IONS,), jnp.float32, math.log(0.1), math.log(1.0))), 0.1, 1.0),
    }


INV_STEP = 0.05
EPSILON = 1e-6


def later(value, axis):
    size = value.shape[axis]
    padded = jnp.pad(value, [(0, 1) if k == axis else (0, 0) for k in range(value.ndim)])
    return lax.slice_in_dim(padded, 1, size + 1, axis=axis)


def earlier(value, axis):
    size = value.shape[axis]
    padded = jnp.pad(value, [(1, 0) if k == axis else (0, 0) for k in range(value.ndim)])
    return lax.slice_in_dim(padded, 0, size, axis=axis)


def plain_sum(value):
    total = later(value, 0) + earlier(value, 0)
    total = total + later(value, 1)
    total = total + earlier(value, 1)
    total = total + later(value, 2)
    total = total + earlier(value, 2)
    return total


def split_sum(current, frozen, upper_x, lower_x, upper_y, lower_y):
    total = jnp.where(upper_x, later(frozen, 0), later(current, 0)) + jnp.where(lower_x, earlier(frozen, 0), earlier(current, 0))
    total = total + jnp.where(upper_y, later(frozen, 1), later(current, 1))
    total = total + jnp.where(lower_y, earlier(frozen, 1), earlier(current, 1))
    total = total + later(current, 2)
    total = total + earlier(current, 2)
    return total


def block_sum(value):
    n_one, n_two, n_three = value.shape
    shaped = value.reshape(n_one // COARSEN, COARSEN, n_two // COARSEN, COARSEN, n_three // COARSEN, COARSEN)
    return shaped.sum(axis=(1, 3, 5))


def reference(state, source, conductance, rebar_cover, colour, diffusivity, binding):
    xs = jnp.arange(NX, dtype=jnp.int32)
    ys = jnp.arange(NY, dtype=jnp.int32)
    zs = jnp.arange(NZ, dtype=jnp.int32)
    upper_x = (xs % CX == CX - 1)[:, None, None]
    lower_x = (xs % CX == 0)[:, None, None]
    upper_y = (ys % CY == CY - 1)[None, :, None]
    lower_y = (ys % CY == 0)[None, :, None]
    parity = (xs[:, None, None] + ys[None, :, None] + zs[None, None, :]) % 2
    owner = jnp.repeat(jnp.repeat(colour, CX, axis=0), CY, axis=1)[:, :, None]
    cover = rebar_cover.astype(jnp.float32)
    cond_sum = block_sum(conductance)

    def one_ion(items):
        conc, supply, spread, strength = items
        coef = spread * conductance
        bound_term = cover * strength * conc / (1.0 + conc)
        mass = INV_STEP + cover * strength / ((1.0 + conc) * (1.0 + conc))
        diag = mass + 6.0 * coef
        rhs = supply - (coef * (6.0 * conc - plain_sum(conc)) + bound_term)
        delta = jnp.zeros_like(conc)
        for phase in range(2):
            frozen = delta
            active = owner == phase
            for sweep in range(SWEEPS):
                for side in range(2):
                    total = split_sum(delta, frozen, upper_x, lower_x, upper_y, lower_y)
                    fresh = (rhs + coef * total) / diag
                    delta = jnp.where(active & (parity == side), fresh, delta)
        fine = rhs - (diag * delta - coef * plain_sum(delta))
        coarse_rhs = block_sum(fine)
        coarse_off = spread * cond_sum / COARSEN
        coarse_diag = block_sum(mass) + 6.0 * coarse_off

        def jacobi(step, value):
            return (coarse_rhs + coarse_off * plain_sum(value)) / coarse_diag

        coarse = lax.fori_loop(0, COARSE_ITERS, jacobi, jnp.zeros_like(coarse_rhs))
        lift = jnp.repeat(jnp.repeat(jnp.repeat(coarse, COARSEN, axis=0), COARSEN, axis=1), COARSEN, axis=2)
        image = diag * lift - coef * plain_sum(lift)
        weight = jnp.sum(fine * image) / (jnp.sum(image * image) + EPSILON)
        delta = delta + weight * lift
        final = rhs - (diag * delta - coef * plain_sum(delta))
        return conc + delta, final

    updated, residual = lax.map(one_ion, (state, source, diffusivity, binding))
    return updated, residual
```

```python
import functools

import jax
import jax.numpy as jnp
from jax import lax
from jax.experimental import pallas as pl
from jax.experimental.pallas import tpu as pltpu
from jax.sharding import PartitionSpec as P

COARSEN = 8
SWEEPS = 4
COARSE_ITERS = 20
INV_STEP = 0.05
EPSILON = 1e-06
MESH = pl.DeviceIdType.MESH
F32 = jnp.float32


def kernel(
    n_span, n_width, ions, cx, cy, cz,
    state_ref, source_ref, cond_ref, cover_ref, colour_ref, spread_ref, strength_ref,
    up_ref, res_ref,
    xs, xh, ys, yh, gath, part, condp, coverp, rhs, diag, c, a, d, image,
    mx, fx, cx_sum, aj, cj, ej, sp, wv,
    send_sem, recv_sem, gsend, grecv, psend, precv,
):
    s = lax.axis_index("span")
    w = lax.axis_index("width")
    total_dev = n_span * n_width
    me = s * n_width + w
    kp = cx // 2
    rows = cy // COARSEN
    row = lax.broadcasted_iota(jnp.int32, (cy, cz), 0)
    lane = lax.broadcasted_iota(jnp.int32, (cy, cz), 1)
    p = (row + lane) % 2 == 1
    first_y, last_y = row == 0, row == cy - 1
    first_z, last_z = lane == 0, lane == cz - 1

    barrier = pltpu.get_barrier_semaphore()

    def partner(off):
        other = lax.rem(me + off, total_dev)
        return (other // n_width, other % n_width)

    @pl.loop(1, total_dev)
    def _(off):
        pl.semaphore_signal(barrier, inc=1, device_id=partner(off), device_id_type=MESH)

    def split(x):
        pairs = x.reshape(kp, 2, cy, cz)
        even, odd = pairs[:, 0], pairs[:, 1]
        return jnp.where(p, odd, even), jnp.where(p, even, odd)

    def yz_sum(v):
        out = jnp.where(last_y, 0.0, pltpu.roll(v, cy - 1, v.ndim - 2))
        out += jnp.where(first_y, 0.0, pltpu.roll(v, 1, v.ndim - 2))
        out += jnp.where(last_z, 0.0, pltpu.roll(v, cz - 1, v.ndim - 1))
        out += jnp.where(first_z, 0.0, pltpu.roll(v, 1, v.ndim - 1))
        return out

    zero_face = jnp.zeros((1, cy, cz), F32)

    def nb_red(black):
        above = jnp.concatenate([black[1:], zero_face], axis=0)
        below = jnp.concatenate([zero_face, black[:-1]], axis=0)
        return black + jnp.where(p, above, below) + yz_sum(black)

    def nb_black(red):
        above = jnp.concatenate([red[1:], zero_face], axis=0)
        below = jnp.concatenate([zero_face, red[:-1]], axis=0)
        return red + jnp.where(p, below, above) + yz_sum(red)

    def rim(e, i):
        lo, hi = xh[e, 0, i], xh[e, 1, i]
        ylo, yhi = yh[e, 0, i], yh[e, 1, i]
        mid = jnp.zeros((kp - 2, cy, cz), F32)

        def faces(k0, k1, half):
            x_part = jnp.concatenate([k0[None], mid, k1[None]], axis=0)
            low = ylo[half * kp:(half + 1) * kp][:, None, :]
            high = yhi[half * kp:(half + 1) * kp][:, None, :]
            return x_part + jnp.where(first_y, low, 0.0) + jnp.where(last_y, high, 0.0)

        red = faces(jnp.where(p, 0.0, lo), jnp.where(p, hi, 0.0), 1)
        black = faces(jnp.where(p, lo, 0.0), jnp.where(p, 0.0, hi), 0)
        return red, black

    def put_y(e, i, red, black):
        ys[e, 0, i] = jnp.concatenate([red[:, cy - 1, :], black[:, cy - 1, :]], axis=0)
        ys[e, 1, i] = jnp.concatenate([red[:, 0, :], black[:, 0, :]], axis=0)

    def put_x(e, i, red, black):
        xs[e - 1, 0, i] = jnp.where(p, red[kp - 1], black[kp - 1])
        xs[e - 1, 1, i] = jnp.where(p, black[0], red[0])

    has = (s < n_span - 1, s > 0, w < n_width - 1, w > 0)
    gets = (s > 0, s < n_span - 1, w > 0, w < n_width - 1)
    to = ((s + 1, w), (s - 1, w), (s, w + 1), (s, w - 1))

    def copy(e, k):
        if k >= 2:
            src, dst = ys.at[e, k - 2], yh.at[e, k - 2]
        else:
            dst = xh.at[e, k]
            if e == 0:
                src = state_ref.at[:, cx - 1] if k == 0 else state_ref.at[:, 0]
            else:
                src = xs.at[e - 1, k]
        return pltpu.make_async_remote_copy(
            src_ref=src, dst_ref=dst, send_sem=send_sem.at[e, k], recv_sem=recv_sem.at[e, k],
            device_id=to[k], device_id_type=MESH,
        )

    def send(e, which):
        for k in which:
            @pl.when(has[k])
            def _():
                copy(e, k).start()

    def receive(e):
        for k in range(4):
            @pl.when(gets[k])
            def _():
                copy(e, k).wait_recv()

    for k in range(4):
        @pl.when(jnp.logical_not(gets[k]))
        def _():
            for e in range(3):
                if k >= 2:
                    yh[e, k - 2] = jnp.zeros(yh.shape[2:], F32)
                else:
                    xh[e, k] = jnp.zeros(xh.shape[2:], F32)

    def pack_state(i, _):
        put_y(0, i, *split(state_ref[i]))
        return 0

    lax.fori_loop(0, ions, pack_state, 0)
    pl.semaphore_wait(barrier, total_dev - 1)
    send(0, range(4))

    condp[0], condp[1] = split(cond_ref[...])
    coverp[0], coverp[1] = split(cover_ref[...].astype(F32))
    cx_sum[...] = jnp.sum(cond_ref[...], axis=0)

    def local_terms(i, _):
        spread, strength = spread_ref[i], strength_ref[i]
        st = split(state_ref[i])
        src = split(source_ref[i])
        near = (nb_red(st[1]), nb_black(st[0]))
        mass_sum = jnp.zeros((cy, cz), F32)
        for h in range(2):
            coef = spread * condp[h]
            inv = 1.0 / (1.0 + st[h])
            bound = coverp[h] * strength * inv
            mass = INV_STEP + bound * inv
            dg = mass + 6.0 * coef
            diag[h, i] = dg
            c[h, i] = coef / dg
            rhs[h, i] = src[h] - (coef * (6.0 * st[h] - near[h]) + bound * st[h])
            mass_sum += jnp.sum(mass, axis=0)
        mx[i] = mass_sum
        return 0

    lax.fori_loop(0, ions, local_terms, 0)
    receive(0)

    mine = colour_ref[0, 0].astype(F32)

    def sweeps(ar, ab, cr, cb):
        red = ar
        black = ab + cb * nb_black(red)
        for _ in range(SWEEPS - 1):
            red = ar + cr * nb_red(black)
            black = ab + cb * nb_black(red)
        return red, black

    def phase_zero(i, _):
        near = rim(0, i)
        for h in range(2):
            right = rhs[h, i] + spread_ref[i] * condp[h] * near[h]
            rhs[h, i] = right
            a[h, i] = right / diag[h, i]
        red, black = sweeps(
            (1.0 - mine) * a[0, i], (1.0 - mine) * a[1, i], c[0, i], c[1, i]
        )
        d[0, i], d[1, i] = red, black
        put_y(1, i, red, black)
        put_x(1, i, red, black)
        return 0

    lax.fori_loop(0, ions, phase_zero, 0)
    send(1, range(4))
    receive(1)

    def phase_one(i, _):
        near = rim(1, i)
        red, black = sweeps(
            mine * (a[0, i] + c[0, i] * near[0]), mine * (a[1, i] + c[1, i] * near[1]),
            c[0, i], c[1, i],
        )
        red, black = red + d[0, i], black + d[1, i]
        d[0, i], d[1, i] = red, black
        put_y(2, i, red, black)
        put_x(2, i, red, black)
        return 0

    lax.fori_loop(0, ions, phase_one, 0)
    send(2, range(4))

    eighth = lane % COARSEN

    def coarse_pack(parts):
        acc = jnp.zeros((cy, cz), F32)
        for i in range(ions):
            v = parts[i]
            for step in (1, 2, 4):
                v = v + pltpu.roll(v, cz - step, 1)
            if i:
                v = pltpu.roll(v, i, 1)
            acc = jnp.where(eighth == i, v, acc)
        return jnp.concatenate(
            [jnp.sum(acc[j * COARSEN:(j + 1) * COARSEN], axis=0, keepdims=True)
             for j in range(rows)], axis=0)

    cond_sum = cx_sum[...]
    coarse_off = coarse_pack([spread_ref[i] * cond_sum for i in range(ions)]) / COARSEN
    coarse_diag = coarse_pack([mx[i] for i in range(ions)]) + 6.0 * coarse_off
    coarse_inv = 1.0 / jnp.where(eighth[:rows] < ions, coarse_diag, 1.0)

    receive(2)

    def fine_terms(i, _):
        near = rim(2, i)
        red, black = d[0, i], d[1, i]
        near = (near[0] + nb_red(black), near[1] + nb_black(red))
        total = jnp.zeros((cy, cz), F32)
        for h, v in ((0, red), (1, black)):
            fine = rhs[h, i] - (diag[h, i] * v - spread_ref[i] * condp[h] * near[h])
            rhs[h, i] = fine
            total += jnp.sum(fine, axis=0)
        fx[i] = total
        return 0

    lax.fori_loop(0, ions, fine_terms, 0)
    crhs = coarse_pack([fx[i] for i in range(ions)])
    gath[me] = jnp.concatenate([crhs * coarse_inv, coarse_off * coarse_inv], axis=0)

    def spread_out(buf, ssem, rsem):
        @pl.loop(1, total_dev)
        def _(off):
            pltpu.make_async_remote_copy(
                src_ref=buf.at[me], dst_ref=buf.at[me], send_sem=ssem, recv_sem=rsem,
                device_id=partner(off), device_id_type=MESH,
            ).start()

    def all_of(buf, sem):
        others = buf.at[pl.ds(0, total_dev - 1)]
        pltpu.make_async_copy(others, others, sem).wait()

    spread_out(gath, gsend, grecv)
    all_of(gath, grecv)

    wide = n_width * rows
    g = gath[...].reshape(n_span, n_width, 2 * rows, cz)
    aj[...] = jnp.concatenate([g[:, k, :rows] for k in range(n_width)], axis=1)
    cj[...] = jnp.concatenate([g[:, k, rows:] for k in range(n_width)], axis=1)
    crow = lax.broadcasted_iota(jnp.int32, (wide, cz), 0)
    clane = lax.broadcasted_iota(jnp.int32, (wide, cz), 1)
    zero_c = jnp.zeros((1, wide, cz), F32)

    def jacobi(_, e):
        total = jnp.concatenate([e[1:], zero_c], axis=0)
        total += jnp.concatenate([zero_c, e[:-1]], axis=0)
        total += jnp.where(crow == wide - 1, 0.0, pltpu.roll(e, wide - 1, 1))
        total += jnp.where(crow == 0, 0.0, pltpu.roll(e, 1, 1))
        total += jnp.where(clane >= cz - COARSEN, 0.0, pltpu.roll(e, cz - COARSEN, 2))
        total += jnp.where(clane < COARSEN, 0.0, pltpu.roll(e, COARSEN, 2))
        return aj[...] + cj[...] * total

    e = lax.fori_loop(0, COARSE_ITERS - 1, jacobi, aj[...])
    ej[0] = zero_c[0]
    ej[n_span + 1] = zero_c[0]
    ej[1:n_span + 1] = e
    before, here, after = ej[s], ej[s + 1], ej[s + 2]

    def own_rows(v):
        out = v[:rows]
        for k in range(1, n_width):
            out = jnp.where(w == k, v[k * rows:(k + 1) * rows], out)
        return out

    y_low = jnp.zeros((1, cz), F32)
    y_high = jnp.zeros((1, cz), F32)
    for k in range(n_width):
        if k > 0:
            y_low = jnp.where(w == k, here[k * rows - 1:k * rows], y_low)
        if k < n_width - 1:
            y_high = jnp.where(w == k, here[(k + 1) * rows:(k + 1) * rows + 1], y_high)
    packed = jnp.concatenate(
        [own_rows(here), own_rows(before), own_rows(after), y_low, y_high,
         jnp.zeros((16 - 3 * rows - 2, cz), F32)], axis=0)
    for i in range(ions):
        v = jnp.where(eighth[:16] == i, packed, 0.0)
        if i:
            v = pltpu.roll(v, cz - i, 1)
        for step in (1, 2, 4):
            v = v + pltpu.roll(v, step, 1)
        sp[i] = v

    def tall(v):
        return jnp.concatenate(
            [jnp.broadcast_to(v[j:j + 1], (COARSEN, cz)) for j in range(rows)], axis=0)

    sums = []
    for i in range(ions):
        v = sp[i]
        lift = tall(v[:rows])
        lo, hi = tall(v[rows:2 * rows]), tall(v[2 * rows:3 * rows])
        base = yz_sum(lift) + lift
        base += jnp.where(first_y, v[3 * rows:3 * rows + 1], 0.0)
        base += jnp.where(last_y, v[3 * rows + 1:3 * rows + 2], 0.0)
        numer = jnp.zeros((cy, cz), F32)
        denom = jnp.zeros((cy, cz), F32)
        for h in range(2):
            for k in range(kp):
                side = lift
                low_side = p if h else jnp.logical_not(p)
                high_side = jnp.logical_not(p) if h else p
                if k == 0:
                    side = jnp.where(low_side, lo, side)
                if k == kp - 1:
                    side = jnp.where(high_side, hi, side)
                im = diag[h, i, k] * lift - spread_ref[i] * condp[h, k] * (base + side)
                image[h, i, k] = im
                numer += rhs[h, i, k] * im
                denom += im * im
        sums.append((jnp.sum(numer, axis=0, keepdims=True), jnp.sum(denom, axis=0, keepdims=True)))
    part[me] = jnp.concatenate([n for n, _ in sums] + [m for _, m in sums], axis=0)
    spread_out(part, psend, precv)
    all_of(part, precv)
    whole = jnp.sum(jnp.sum(part[...], axis=0), axis=1, keepdims=True)
    weight = whole[:ions] / (whole[ions:] + EPSILON)
    wv[...] = jnp.broadcast_to(weight, (ions, cz))

    for i in range(ions):
        wt = wv[i:i + 1]
        lifted = wt * tall(sp[i, :rows])
        for k in range(kp):
            red, black = d[0, i, k], d[1, i, k]
            up_ref[i, 2 * k] = state_ref[i, 2 * k] + (jnp.where(p, black, red) + lifted)
            up_ref[i, 2 * k + 1] = state_ref[i, 2 * k + 1] + (jnp.where(p, red, black) + lifted)
            red = rhs[0, i, k] - wt * image[0, i, k]
            black = rhs[1, i, k] - wt * image[1, i, k]
            res_ref[i, 2 * k] = jnp.where(p, black, red)
            res_ref[i, 2 * k + 1] = jnp.where(p, red, black)

    for e in range(3):
        for k in range(4):
            @pl.when(has[k])
            def _():
                copy(e, k).wait_send()
    all_of(gath, gsend)
    all_of(part, psend)


def on_device(n_span, n_width, state, source, conductance, rebar_cover, colour, diffusivity, binding):
    ions, cx, cy, cz = state.shape
    kp = cx // 2
    total = n_span * n_width
    rows = cy // COARSEN
    half = pltpu.VMEM((2, ions, kp, cy, cz), F32)
    pair = pltpu.VMEM((2, kp, cy, cz), F32)
    vmem = pl.BlockSpec(memory_space=pltpu.VMEM)
    smem = pl.BlockSpec(memory_space=pltpu.SMEM)
    dma = pltpu.SemaphoreType.DMA
    return pl.pallas_call(
        functools.partial(kernel, n_span, n_width, ions, cx, cy, cz),
        out_shape=(jax.ShapeDtypeStruct(state.shape, F32),) * 2,
        in_specs=[vmem] * 4 + [smem] * 3,
        out_specs=(vmem, vmem),
        scratch_shapes=[
            pltpu.VMEM((2, 2, ions, cy, cz), F32),
            pltpu.VMEM((3, 2, ions, cy, cz), F32),
            pltpu.VMEM((3, 2, ions, 2 * kp, cz), F32),
            pltpu.VMEM((3, 2, ions, 2 * kp, cz), F32),
            pltpu.VMEM((total, 2 * rows, cz), F32),
            pltpu.VMEM((total, 2 * ions, cz), F32),
            pair, pair, half, half, half, half, half, half,
            pltpu.VMEM((ions, cy, cz), F32),
            pltpu.VMEM((ions, cy, cz), F32),
            pltpu.VMEM((cy, cz), F32),
            pltpu.VMEM((n_span, n_width * rows, cz), F32),
            pltpu.VMEM((n_span, n_width * rows, cz), F32),
            pltpu.VMEM((n_span + 2, n_width * rows, cz), F32),
            pltpu.VMEM((ions, 16, cz), F32),
            pltpu.VMEM((ions, cz), F32),
            dma((3, 4)), dma((3, 4)), dma, dma, dma, dma,
        ],
        compiler_params=pltpu.CompilerParams(
            collective_id=0, has_side_effects=True, vmem_limit_bytes=40 * 1024 * 1024
        ),
    )(state, source, conductance, rebar_cover, colour, diffusivity, binding)


def solution(mesh):
    in_specs = (
        P(None, "span", "width", None),
        P(None, "span", "width", None),
        P("span", "width", None),
        P("span", "width", None),
        P("span", "width"),
        P(),
        P(),
    )
    out_specs = (P(None, "span", "width", None), P(None, "span", "width", None))
    return jax.shard_map(
        functools.partial(on_device, mesh.shape["span"], mesh.shape["width"]),
        mesh=mesh, in_specs=in_specs, out_specs=out_specs, check_vma=False,
    )
```

```python
import functools

import jax
import jax.numpy as jnp
from jax import lax
from jax.experimental import pallas as pl
from jax.experimental.pallas import tpu as pltpu
from jax.sharding import PartitionSpec as P

COARSEN = 8
SWEEPS = 4
COARSE_ITERS = 20
INV_STEP = 0.05
EPSILON = 1e-06
MESH = pl.DeviceIdType.MESH
F32 = jnp.float32


def kernel(
    n_span, n_width, ions, cx, cy, cz,
    state_hbm, source_hbm, cond_hbm, cover_hbm, colour_ref, spread_ref, strength_ref,
    up_ref, res_ref,
    state_ref, source_ref, cond_ref, cover_ref, xs, xh, ys, yh, first, gath, second, part, condp, coverp, rhs, diag, c, a, d, image,
    mx, fx, cx_sum, aj, cj, ej, sp, wv,
    send_sem, recv_sem, gsend, grecv, psend, precv, in_sem,
):
    s = lax.axis_index("span")
    w = lax.axis_index("width")
    kp = cx // 2
    rows = cy // COARSEN
    row = lax.broadcasted_iota(jnp.int32, (cy, cz), 0)
    lane = lax.broadcasted_iota(jnp.int32, (cy, cz), 1)
    p = (row + lane) % 2 == 1
    first_y, last_y = row == 0, row == cy - 1
    first_z, last_z = lane == 0, lane == cz - 1

    loads = [
        pltpu.make_async_copy(src, dst, in_sem.at[k])
        for k, (src, dst) in enumerate((
            (state_hbm, state_ref), (cond_hbm, cond_ref),
            (cover_hbm, cover_ref), (source_hbm, source_ref)))
    ]
    for load in loads:
        load.start()

    barrier = pltpu.get_barrier_semaphore()

    for off in range(1, n_width):
        pl.semaphore_signal(
            barrier, inc=1, device_id=(s, lax.rem(w + off, n_width)), device_id_type=MESH)

    @pl.loop(1, n_span)
    def _(off):
        pl.semaphore_signal(
            barrier, inc=1, device_id=(lax.rem(s + off, n_span), w), device_id_type=MESH)

    def split(x):
        pairs = x.reshape(kp, 2, cy, cz)
        even, odd = pairs[:, 0], pairs[:, 1]
        return jnp.where(p, odd, even), jnp.where(p, even, odd)

    def yz_sum(v):
        out = jnp.where(last_y, 0.0, pltpu.roll(v, cy - 1, v.ndim - 2))
        out += jnp.where(first_y, 0.0, pltpu.roll(v, 1, v.ndim - 2))
        out += jnp.where(last_z, 0.0, pltpu.roll(v, cz - 1, v.ndim - 1))
        out += jnp.where(first_z, 0.0, pltpu.roll(v, 1, v.ndim - 1))
        return out

    zero_face = jnp.zeros((1, cy, cz), F32)

    def nb_red(black):
        above = jnp.concatenate([black[1:], zero_face], axis=0)
        below = jnp.concatenate([zero_face, black[:-1]], axis=0)
        return black + jnp.where(p, above, below) + yz_sum(black)

    def nb_black(red):
        above = jnp.concatenate([red[1:], zero_face], axis=0)
        below = jnp.concatenate([zero_face, red[:-1]], axis=0)
        return red + jnp.where(p, below, above) + yz_sum(red)

    def rim(e, i):
        lo, hi = xh[e, 0, i], xh[e, 1, i]
        ylo, yhi = yh[e, 0, i], yh[e, 1, i]
        mid = jnp.zeros((kp - 2, cy, cz), F32)

        def faces(k0, k1, half):
            x_part = jnp.concatenate([k0[None], mid, k1[None]], axis=0)
            low = ylo[half * kp:(half + 1) * kp][:, None, :]
            high = yhi[half * kp:(half + 1) * kp][:, None, :]
            return x_part + jnp.where(first_y, low, 0.0) + jnp.where(last_y, high, 0.0)

        red = faces(jnp.where(p, 0.0, lo), jnp.where(p, hi, 0.0), 1)
        black = faces(jnp.where(p, lo, 0.0), jnp.where(p, 0.0, hi), 0)
        return red, black

    def put_y(e, i, red, black):
        ys[e, 0, i] = jnp.concatenate([red[:, cy - 1, :], black[:, cy - 1, :]], axis=0)
        ys[e, 1, i] = jnp.concatenate([red[:, 0, :], black[:, 0, :]], axis=0)

    def put_x(e, i, red, black):
        xs[e - 1, 0, i] = jnp.where(p, red[kp - 1], black[kp - 1])
        xs[e - 1, 1, i] = jnp.where(p, black[0], red[0])

    has = (s < n_span - 1, s > 0, w < n_width - 1, w > 0)
    gets = (s > 0, s < n_span - 1, w > 0, w < n_width - 1)
    to = ((s + 1, w), (s - 1, w), (s, w + 1), (s, w - 1))

    def copy(e, k):
        if k >= 2:
            src, dst = ys.at[e, k - 2], yh.at[e, k - 2]
        else:
            dst = xh.at[e, k]
            if e == 0:
                src = state_ref.at[:, cx - 1] if k == 0 else state_ref.at[:, 0]
            else:
                src = xs.at[e - 1, k]
        return pltpu.make_async_remote_copy(
            src_ref=src, dst_ref=dst, send_sem=send_sem.at[e, k], recv_sem=recv_sem.at[e, k],
            device_id=to[k], device_id_type=MESH,
        )

    def send(e, which):
        for k in which:
            @pl.when(has[k])
            def _():
                copy(e, k).start()

    def receive(e):
        for k in range(4):
            @pl.when(gets[k])
            def _():
                copy(e, k).wait_recv()

    for k in range(4):
        @pl.when(jnp.logical_not(gets[k]))
        def _():
            for e in range(3):
                if k >= 2:
                    yh[e, k - 2] = jnp.zeros(yh.shape[2:], F32)
                else:
                    xh[e, k] = jnp.zeros(xh.shape[2:], F32)

    def pack_state(i, _):
        put_y(0, i, *split(state_ref[i]))
        return 0

    loads[0].wait()
    lax.fori_loop(0, ions, pack_state, 0)
    pl.semaphore_wait(barrier, n_span + n_width - 2)
    send(0, range(4))

    for load in loads[1:]:
        load.wait()
    condp[0], condp[1] = split(cond_ref[...])
    coverp[0], coverp[1] = split(cover_ref[...].astype(F32))
    cx_sum[...] = jnp.sum(cond_ref[...], axis=0)

    def local_terms(i, _):
        spread, strength = spread_ref[i], strength_ref[i]
        st = split(state_ref[i])
        src = split(source_ref[i])
        near = (nb_red(st[1]), nb_black(st[0]))
        mass_sum = jnp.zeros((cy, cz), F32)
        for h in range(2):
            coef = spread * condp[h]
            inv = 1.0 / (1.0 + st[h])
            bound = coverp[h] * strength * inv
            mass = INV_STEP + bound * inv
            dg = mass + 6.0 * coef
            diag[h, i] = dg
            c[h, i] = coef / dg
            rhs[h, i] = src[h] - (coef * (6.0 * st[h] - near[h]) + bound * st[h])
            mass_sum += jnp.sum(mass, axis=0)
        mx[i] = mass_sum
        return 0

    lax.fori_loop(0, ions, local_terms, 0)
    receive(0)

    mine = colour_ref[0, 0].astype(F32)

    def sweeps(ar, ab, cr, cb):
        red = ar
        black = ab + cb * nb_black(red)
        for _ in range(SWEEPS - 1):
            red = ar + cr * nb_red(black)
            black = ab + cb * nb_black(red)
        return red, black

    def phase_zero(i, _):
        near = rim(0, i)
        for h in range(2):
            right = rhs[h, i] + spread_ref[i] * condp[h] * near[h]
            rhs[h, i] = right
            a[h, i] = right / diag[h, i]
        red, black = sweeps(
            (1.0 - mine) * a[0, i], (1.0 - mine) * a[1, i], c[0, i], c[1, i]
        )
        d[0, i], d[1, i] = red, black
        put_y(1, i, red, black)
        put_x(1, i, red, black)
        return 0

    lax.fori_loop(0, ions, phase_zero, 0, unroll=2)
    send(1, range(4))
    receive(1)

    def phase_one(i, _):
        near = rim(1, i)
        red, black = sweeps(
            mine * (a[0, i] + c[0, i] * near[0]), mine * (a[1, i] + c[1, i] * near[1]),
            c[0, i], c[1, i],
        )
        red, black = red + d[0, i], black + d[1, i]
        d[0, i], d[1, i] = red, black
        put_y(2, i, red, black)
        put_x(2, i, red, black)
        return 0

    lax.fori_loop(0, ions, phase_one, 0, unroll=2)
    send(2, range(4))

    eighth = lane % COARSEN

    def coarse_pack(parts):
        acc = jnp.zeros((cy, cz), F32)
        for i in range(ions):
            v = parts[i]
            for step in (1, 2, 4):
                v = v + pltpu.roll(v, cz - step, 1)
            if i:
                v = pltpu.roll(v, i, 1)
            acc = jnp.where(eighth == i, v, acc)
        return jnp.concatenate(
            [jnp.sum(acc[j * COARSEN:(j + 1) * COARSEN], axis=0, keepdims=True)
             for j in range(rows)], axis=0)

    cond_sum = cx_sum[...]
    coarse_off = coarse_pack([spread_ref[i] * cond_sum for i in range(ions)]) / COARSEN
    coarse_diag = coarse_pack([mx[i] for i in range(ions)]) + 6.0 * coarse_off
    coarse_inv = 1.0 / jnp.where(eighth[:rows] < ions, coarse_diag, 1.0)

    receive(2)

    def fine_terms(i, _):
        near = rim(2, i)
        red, black = d[0, i], d[1, i]
        near = (near[0] + nb_red(black), near[1] + nb_black(red))
        total = jnp.zeros((cy, cz), F32)
        for h, v in ((0, red), (1, black)):
            fine = rhs[h, i] - (diag[h, i] * v - spread_ref[i] * condp[h] * near[h])
            rhs[h, i] = fine
            total += jnp.sum(fine, axis=0)
        fx[i] = total
        return 0

    lax.fori_loop(0, ions, fine_terms, 0)
    crhs = coarse_pack([fx[i] for i in range(ions)])
    first[w] = jnp.concatenate([crhs * coarse_inv, coarse_off * coarse_inv], axis=0)

    def to_row(buf, ssem, rsem):
        for off in range(1, n_width):
            pltpu.make_async_remote_copy(
                src_ref=buf.at[w], dst_ref=buf.at[w], send_sem=ssem, recv_sem=rsem,
                device_id=(s, lax.rem(w + off, n_width)), device_id_type=MESH,
            ).start()

    def to_column(buf, ssem, rsem):
        @pl.loop(1, n_span)
        def _(off):
            pltpu.make_async_remote_copy(
                src_ref=buf.at[s], dst_ref=buf.at[s], send_sem=ssem, recv_sem=rsem,
                device_id=(lax.rem(s + off, n_span), w), device_id_type=MESH,
            ).start()

    def all_of(buf, sem, count):
        others = buf.at[pl.ds(0, count - 1)]
        pltpu.make_async_copy(others, others, sem).wait()

    to_row(first, gsend.at[0], grecv.at[0])
    all_of(first, grecv.at[0], n_width)
    gath[s] = first[...]
    to_column(gath, gsend.at[1], grecv.at[1])
    all_of(gath, grecv.at[1], n_span)

    wide = n_width * rows
    g = gath[...]
    aj[...] = jnp.concatenate([g[:, k, :rows] for k in range(n_width)], axis=1)
    cj[...] = jnp.concatenate([g[:, k, rows:] for k in range(n_width)], axis=1)
    crow = lax.broadcasted_iota(jnp.int32, (wide, cz), 0)
    clane = lax.broadcasted_iota(jnp.int32, (wide, cz), 1)
    zero_c = jnp.zeros((1, wide, cz), F32)

    def jacobi(_, e):
        total = jnp.concatenate([e[1:], zero_c], axis=0)
        total += jnp.concatenate([zero_c, e[:-1]], axis=0)
        total += jnp.where(crow == wide - 1, 0.0, pltpu.roll(e, wide - 1, 1))
        total += jnp.where(crow == 0, 0.0, pltpu.roll(e, 1, 1))
        total += jnp.where(clane >= cz - COARSEN, 0.0, pltpu.roll(e, cz - COARSEN, 2))
        total += jnp.where(clane < COARSEN, 0.0, pltpu.roll(e, COARSEN, 2))
        return aj[...] + cj[...] * total

    e = lax.fori_loop(0, COARSE_ITERS - 1, jacobi, aj[...])
    ej[0] = zero_c[0]
    ej[n_span + 1] = zero_c[0]
    ej[1:n_span + 1] = e
    before, here, after = ej[s], ej[s + 1], ej[s + 2]

    def own_rows(v):
        out = v[:rows]
        for k in range(1, n_width):
            out = jnp.where(w == k, v[k * rows:(k + 1) * rows], out)
        return out

    y_low = jnp.zeros((1, cz), F32)
    y_high = jnp.zeros((1, cz), F32)
    for k in range(n_width):
        if k > 0:
            y_low = jnp.where(w == k, here[k * rows - 1:k * rows], y_low)
        if k < n_width - 1:
            y_high = jnp.where(w == k, here[(k + 1) * rows:(k + 1) * rows + 1], y_high)
    packed = jnp.concatenate(
        [own_rows(here), own_rows(before), own_rows(after), y_low, y_high,
         jnp.zeros((16 - 3 * rows - 2, cz), F32)], axis=0)
    for i in range(ions):
        v = jnp.where(eighth[:16] == i, packed, 0.0)
        if i:
            v = pltpu.roll(v, cz - i, 1)
        for step in (1, 2, 4):
            v = v + pltpu.roll(v, step, 1)
        sp[i] = v

    def tall(v):
        return jnp.concatenate(
            [jnp.broadcast_to(v[j:j + 1], (COARSEN, cz)) for j in range(rows)], axis=0)

    sums = []
    for i in range(ions):
        v = sp[i]
        lift = tall(v[:rows])
        lo, hi = tall(v[rows:2 * rows]), tall(v[2 * rows:3 * rows])
        base = yz_sum(lift) + lift
        base += jnp.where(first_y, v[3 * rows:3 * rows + 1], 0.0)
        base += jnp.where(last_y, v[3 * rows + 1:3 * rows + 2], 0.0)
        numer = jnp.zeros((cy, cz), F32)
        denom = jnp.zeros((cy, cz), F32)
        for h in range(2):
            for k in range(kp):
                side = lift
                low_side = p if h else jnp.logical_not(p)
                high_side = jnp.logical_not(p) if h else p
                if k == 0:
                    side = jnp.where(low_side, lo, side)
                if k == kp - 1:
                    side = jnp.where(high_side, hi, side)
                im = diag[h, i, k] * lift - spread_ref[i] * condp[h, k] * (base + side)
                image[h, i, k] = im
                numer += rhs[h, i, k] * im
                denom += im * im
        sums.append((jnp.sum(numer, axis=0, keepdims=True), jnp.sum(denom, axis=0, keepdims=True)))
    second[w] = jnp.concatenate([n for n, _ in sums] + [m for _, m in sums], axis=0)
    to_row(second, psend.at[0], precv.at[0])
    all_of(second, precv.at[0], n_width)
    part[s] = jnp.sum(second[...], axis=0)
    to_column(part, psend.at[1], precv.at[1])
    all_of(part, precv.at[1], n_span)
    whole = jnp.sum(jnp.sum(part[...], axis=0), axis=1, keepdims=True)
    weight = whole[:ions] / (whole[ions:] + EPSILON)
    wv[...] = jnp.broadcast_to(weight, (ions, cz))

    for i in range(ions):
        wt = wv[i:i + 1]
        lifted = wt * tall(sp[i, :rows])
        for k in range(kp):
            red, black = d[0, i, k], d[1, i, k]
            up_ref[i, 2 * k] = state_ref[i, 2 * k] + (jnp.where(p, black, red) + lifted)
            up_ref[i, 2 * k + 1] = state_ref[i, 2 * k + 1] + (jnp.where(p, red, black) + lifted)
            red = rhs[0, i, k] - wt * image[0, i, k]
            black = rhs[1, i, k] - wt * image[1, i, k]
            res_ref[i, 2 * k] = jnp.where(p, black, red)
            res_ref[i, 2 * k + 1] = jnp.where(p, red, black)

    for e in range(3):
        for k in range(4):
            @pl.when(has[k])
            def _():
                copy(e, k).wait_send()
    all_of(first, gsend.at[0], n_width)
    all_of(gath, gsend.at[1], n_span)
    all_of(second, psend.at[0], n_width)
    all_of(part, psend.at[1], n_span)


def on_device(n_span, n_width, state, source, conductance, rebar_cover, colour, diffusivity, binding):
    ions, cx, cy, cz = state.shape
    kp = cx // 2
    rows = cy // COARSEN
    half = pltpu.VMEM((2, ions, kp, cy, cz), F32)
    pair = pltpu.VMEM((2, kp, cy, cz), F32)
    vmem = pl.BlockSpec(memory_space=pltpu.VMEM)
    smem = pl.BlockSpec(memory_space=pltpu.SMEM)
    dma = pltpu.SemaphoreType.DMA
    return pl.pallas_call(
        functools.partial(kernel, n_span, n_width, ions, cx, cy, cz),
        out_shape=(jax.ShapeDtypeStruct(state.shape, F32),) * 2,
        in_specs=[pl.BlockSpec(memory_space=pltpu.HBM)] * 4 + [smem] * 3,
        out_specs=(vmem, vmem),
        scratch_shapes=[
            pltpu.VMEM(state.shape, F32), pltpu.VMEM(state.shape, F32),
            pltpu.VMEM(conductance.shape, F32), pltpu.VMEM(conductance.shape, jnp.int32),
            pltpu.VMEM((2, 2, ions, cy, cz), F32),
            pltpu.VMEM((3, 2, ions, cy, cz), F32),
            pltpu.VMEM((3, 2, ions, 2 * kp, cz), F32),
            pltpu.VMEM((3, 2, ions, 2 * kp, cz), F32),
            pltpu.VMEM((n_width, 2 * rows, cz), F32),
            pltpu.VMEM((n_span, n_width, 2 * rows, cz), F32),
            pltpu.VMEM((n_width, 2 * ions, cz), F32),
            pltpu.VMEM((n_span, 2 * ions, cz), F32),
            pair, pair, half, half, half, half, half, half,
            pltpu.VMEM((ions, cy, cz), F32),
            pltpu.VMEM((ions, cy, cz), F32),
            pltpu.VMEM((cy, cz), F32),
            pltpu.VMEM((n_span, n_width * rows, cz), F32),
            pltpu.VMEM((n_span, n_width * rows, cz), F32),
            pltpu.VMEM((n_span + 2, n_width * rows, cz), F32),
            pltpu.VMEM((ions, 16, cz), F32),
            pltpu.VMEM((ions, cz), F32),
            dma((3, 4)), dma((3, 4)), dma((2,)), dma((2,)), dma((2,)), dma((2,)), dma((4,)),
        ],
        compiler_params=pltpu.CompilerParams(
            collective_id=0, has_side_effects=True, vmem_limit_bytes=60 * 1024 * 1024
        ),
    )(state, source, conductance, rebar_cover, colour, diffusivity, binding)


def solution(mesh):
    in_specs = (
        P(None, "span", "width", None),
        P(None, "span", "width", None),
        P("span", "width", None),
        P("span", "width", None),
        P("span", "width"),
        P(),
        P(),
    )
    out_specs = (P(None, "span", "width", None), P(None, "span", "width", None))
    return jax.shard_map(
        functools.partial(on_device, mesh.shape["span"], mesh.shape["width"]),
        mesh=mesh, in_specs=in_specs, out_specs=out_specs, check_vma=False,
    )
```

```python
import functools

import jax
import jax.numpy as jnp
from jax import lax
from jax.experimental import pallas as pl
from jax.experimental.pallas import tpu as pltpu
from jax.sharding import PartitionSpec as P

COARSEN = 8
SWEEPS = 4
COARSE_ITERS = 20
INV_STEP = 0.05
EPSILON = 1e-06
MESH = pl.DeviceIdType.MESH
F32 = jnp.float32


def kernel(
    n_span, n_width, ions, cx, cy, cz,
    state_hbm, source_hbm, cond_hbm, cover_hbm, colour_ref, spread_ref, strength_ref,
    up_ref, res_ref,
    state_ref, source_ref, cond_ref, cover_ref, xs, xh, ys, yh, first, gath, second, part, condp, coverp, rhs, diag, c, a, d, image,
    mx, fx, cx_sum, aj, cj, ej, sp, wv,
    send_sem, recv_sem, gsend, grecv, psend, precv, in_sem, met,
):
    s = lax.axis_index("span")
    w = lax.axis_index("width")
    kp = cx // 2
    rows = cy // COARSEN
    row = lax.broadcasted_iota(jnp.int32, (cy, cz), 0)
    lane = lax.broadcasted_iota(jnp.int32, (cy, cz), 1)
    p = (row + lane) % 2 == 1
    first_y, last_y = row == 0, row == cy - 1
    first_z, last_z = lane == 0, lane == cz - 1

    loads = [
        pltpu.make_async_copy(src, dst, in_sem.at[k])
        for k, (src, dst) in enumerate((
            (state_hbm, state_ref), (cond_hbm, cond_ref),
            (cover_hbm, cover_ref), (source_hbm, source_ref)))
    ]
    for load in loads:
        load.start()

    barrier = pltpu.get_barrier_semaphore()

    has = (s < n_span - 1, s > 0, w < n_width - 1, w > 0)
    gets = (s > 0, s < n_span - 1, w > 0, w < n_width - 1)
    to = ((s + 1, w), (s - 1, w), (s, w + 1), (s, w - 1))

    def flip(v, bit):
        return v + bit - 2 * bit * (v // bit % 2)

    bits = [1 << k for k in range((max(n_span, n_width) - 1).bit_length())]
    hops = [(s, flip(w, b)) for b in bits if b < n_width]
    hops += [(flip(s, b), w) for b in bits if b < n_span]
    far = [(s, flip(w, b)) for b in bits if 1 < b < n_width]
    far += [(flip(s, b), w) for b in bits if 1 < b < n_span]
    for k in range(4):
        @pl.when(has[k])
        def _():
            pl.semaphore_signal(barrier, inc=1, device_id=to[k], device_id_type=MESH)
    for other in far:
        pl.semaphore_signal(barrier, inc=1, device_id=other, device_id_type=MESH)

    def meet(which):
        for k in which:
            if 0 <= k < len(hops):
                pl.semaphore_signal(
                    met.at[k], inc=1, device_id=hops[k], device_id_type=MESH)

    def met_by(which):
        for k in which:
            if 0 <= k < len(hops):
                pl.semaphore_wait(met.at[k], 1)

    def split(x):
        pairs = x.reshape(kp, 2, cy, cz)
        even, odd = pairs[:, 0], pairs[:, 1]
        return jnp.where(p, odd, even), jnp.where(p, even, odd)

    def yz_sum(v):
        out = jnp.where(last_y, 0.0, pltpu.roll(v, cy - 1, v.ndim - 2))
        out += jnp.where(first_y, 0.0, pltpu.roll(v, 1, v.ndim - 2))
        out += jnp.where(last_z, 0.0, pltpu.roll(v, cz - 1, v.ndim - 1))
        out += jnp.where(first_z, 0.0, pltpu.roll(v, 1, v.ndim - 1))
        return out

    zero_face = jnp.zeros((1, cy, cz), F32)

    def nb_red(black):
        above = jnp.concatenate([black[1:], zero_face], axis=0)
        below = jnp.concatenate([zero_face, black[:-1]], axis=0)
        return black + jnp.where(p, above, below) + yz_sum(black)

    def nb_black(red):
        above = jnp.concatenate([red[1:], zero_face], axis=0)
        below = jnp.concatenate([zero_face, red[:-1]], axis=0)
        return red + jnp.where(p, below, above) + yz_sum(red)

    def rim(e, i):
        lo, hi = xh[e, 0, i], xh[e, 1, i]
        ylo, yhi = yh[e, 0, i], yh[e, 1, i]
        mid = jnp.zeros((kp - 2, cy, cz), F32)

        def faces(k0, k1, half):
            x_part = jnp.concatenate([k0[None], mid, k1[None]], axis=0)
            low = ylo[half * kp:(half + 1) * kp][:, None, :]
            high = yhi[half * kp:(half + 1) * kp][:, None, :]
            return x_part + jnp.where(first_y, low, 0.0) + jnp.where(last_y, high, 0.0)

        red = faces(jnp.where(p, 0.0, lo), jnp.where(p, hi, 0.0), 1)
        black = faces(jnp.where(p, lo, 0.0), jnp.where(p, 0.0, hi), 0)
        return red, black

    def put_y(e, i, red, black):
        ys[e, 0, i] = jnp.concatenate([red[:, cy - 1, :], black[:, cy - 1, :]], axis=0)
        ys[e, 1, i] = jnp.concatenate([red[:, 0, :], black[:, 0, :]], axis=0)

    def put_x(e, i, red, black):
        xs[e - 1, 0, i] = jnp.where(p, red[kp - 1], black[kp - 1])
        xs[e - 1, 1, i] = jnp.where(p, black[0], red[0])

    def copy(e, k):
        if k >= 2:
            src, dst = ys.at[e, k - 2], yh.at[e, k - 2]
        else:
            dst = xh.at[e, k]
            if e == 0:
                src = state_ref.at[:, cx - 1] if k == 0 else state_ref.at[:, 0]
            else:
                src = xs.at[e - 1, k]
        return pltpu.make_async_remote_copy(
            src_ref=src, dst_ref=dst, send_sem=send_sem.at[e, k], recv_sem=recv_sem.at[e, k],
            device_id=to[k], device_id_type=MESH,
        )

    def send(e, which):
        for k in which:
            @pl.when(has[k])
            def _():
                copy(e, k).start()

    def receive(e):
        for k in range(4):
            @pl.when(gets[k])
            def _():
                copy(e, k).wait_recv()

    for k in range(4):
        @pl.when(jnp.logical_not(gets[k]))
        def _():
            for e in range(3):
                if k >= 2:
                    yh[e, k - 2] = jnp.zeros(yh.shape[2:], F32)
                else:
                    xh[e, k] = jnp.zeros(xh.shape[2:], F32)

    def pack_state(i, _):
        put_y(0, i, *split(state_ref[i]))
        return 0

    loads[0].wait()
    lax.fori_loop(0, ions, pack_state, 0)
    near = sum(g.astype(jnp.int32) for g in gets)
    pl.semaphore_wait(barrier, near + len(far))
    send(0, range(4))
    meet((0,))

    for load in loads[1:]:
        load.wait()
    condp[0], condp[1] = split(cond_ref[...])
    coverp[0], coverp[1] = split(cover_ref[...].astype(F32))
    cx_sum[...] = jnp.sum(cond_ref[...], axis=0)

    def local_terms(i, _):
        spread, strength = spread_ref[i], strength_ref[i]
        st = split(state_ref[i])
        src = split(source_ref[i])
        near = (nb_red(st[1]), nb_black(st[0]))
        mass_sum = jnp.zeros((cy, cz), F32)
        for h in range(2):
            coef = spread * condp[h]
            inv = 1.0 / (1.0 + st[h])
            bound = coverp[h] * strength * inv
            mass = INV_STEP + bound * inv
            dg = mass + 6.0 * coef
            diag[h, i] = dg
            c[h, i] = coef / dg
            rhs[h, i] = src[h] - (coef * (6.0 * st[h] - near[h]) + bound * st[h])
            mass_sum += jnp.sum(mass, axis=0)
        mx[i] = mass_sum
        return 0

    lax.fori_loop(0, ions, local_terms, 0)
    receive(0)
    met_by((0,))
    meet((1,))

    mine = colour_ref[0, 0].astype(F32)

    def sweeps(ar, ab, cr, cb):
        red = ar
        black = ab + cb * nb_black(red)
        for _ in range(SWEEPS - 1):
            red = ar + cr * nb_red(black)
            black = ab + cb * nb_black(red)
        return red, black

    def phase_zero(i, _):
        near = rim(0, i)
        for h in range(2):
            right = rhs[h, i] + spread_ref[i] * condp[h] * near[h]
            rhs[h, i] = right
            a[h, i] = right / diag[h, i]
        red, black = sweeps(
            (1.0 - mine) * a[0, i], (1.0 - mine) * a[1, i], c[0, i], c[1, i]
        )
        d[0, i], d[1, i] = red, black
        put_y(1, i, red, black)
        put_x(1, i, red, black)
        return 0

    lax.fori_loop(0, ions, phase_zero, 0, unroll=2)
    send(1, range(4))
    met_by((1,))
    meet((2,))
    receive(1)
    met_by((2,))
    meet((3,))

    def phase_one(i, _):
        near = rim(1, i)
        red, black = sweeps(
            mine * (a[0, i] + c[0, i] * near[0]), mine * (a[1, i] + c[1, i] * near[1]),
            c[0, i], c[1, i],
        )
        red, black = red + d[0, i], black + d[1, i]
        d[0, i], d[1, i] = red, black
        put_y(2, i, red, black)
        put_x(2, i, red, black)
        return 0

    lax.fori_loop(0, ions, phase_one, 0, unroll=2)
    send(2, range(4))
    met_by((3,))
    meet((4,))

    eighth = lane % COARSEN

    def coarse_pack(parts):
        acc = jnp.zeros((cy, cz), F32)
        for i in range(ions):
            v = parts[i]
            for step in (1, 2, 4):
                v = v + pltpu.roll(v, cz - step, 1)
            if i:
                v = pltpu.roll(v, i, 1)
            acc = jnp.where(eighth == i, v, acc)
        return jnp.concatenate(
            [jnp.sum(acc[j * COARSEN:(j + 1) * COARSEN], axis=0, keepdims=True)
             for j in range(rows)], axis=0)

    cond_sum = cx_sum[...]
    coarse_off = coarse_pack([spread_ref[i] * cond_sum for i in range(ions)]) / COARSEN
    coarse_diag = coarse_pack([mx[i] for i in range(ions)]) + 6.0 * coarse_off
    coarse_inv = 1.0 / jnp.where(eighth[:rows] < ions, coarse_diag, 1.0)

    receive(2)

    def fine_terms(i, _):
        near = rim(2, i)
        red, black = d[0, i], d[1, i]
        near = (near[0] + nb_red(black), near[1] + nb_black(red))
        total = jnp.zeros((cy, cz), F32)
        for h, v in ((0, red), (1, black)):
            fine = rhs[h, i] - (diag[h, i] * v - spread_ref[i] * condp[h] * near[h])
            rhs[h, i] = fine
            total += jnp.sum(fine, axis=0)
        fx[i] = total
        return 0

    met_by((4,))
    for k in range(5, len(hops)):
        meet((k,))
        met_by((k,))
    lax.fori_loop(0, ions, fine_terms, 0, unroll=2)
    crhs = coarse_pack([fx[i] for i in range(ions)])
    first[w] = jnp.concatenate([crhs * coarse_inv, coarse_off * coarse_inv], axis=0)

    def to_row(buf, ssem, rsem):
        for off in range(1, n_width):
            pltpu.make_async_remote_copy(
                src_ref=buf.at[w], dst_ref=buf.at[w], send_sem=ssem, recv_sem=rsem,
                device_id=(s, lax.rem(w + off, n_width)), device_id_type=MESH,
            ).start()

    def to_column(buf, ssem, rsem):
        @pl.loop(1, n_span)
        def _(off):
            pltpu.make_async_remote_copy(
                src_ref=buf.at[s], dst_ref=buf.at[s], send_sem=ssem, recv_sem=rsem,
                device_id=(lax.rem(s + off, n_span), w), device_id_type=MESH,
            ).start()

    def all_of(buf, sem, count):
        others = buf.at[pl.ds(0, count - 1)]
        pltpu.make_async_copy(others, others, sem).wait()

    to_row(first, gsend.at[0], grecv.at[0])
    all_of(first, grecv.at[0], n_width)
    gath[s] = first[...]
    to_column(gath, gsend.at[1], grecv.at[1])
    all_of(gath, grecv.at[1], n_span)

    wide = n_width * rows
    g = gath[...]
    aj[...] = jnp.concatenate([g[:, k, :rows] for k in range(n_width)], axis=1)
    cj[...] = jnp.concatenate([g[:, k, rows:] for k in range(n_width)], axis=1)
    crow = lax.broadcasted_iota(jnp.int32, (wide, cz), 0)
    clane = lax.broadcasted_iota(jnp.int32, (wide, cz), 1)
    zero_c = jnp.zeros((1, wide, cz), F32)

    def jacobi(_, e):
        total = jnp.concatenate([e[1:], zero_c], axis=0)
        total += jnp.concatenate([zero_c, e[:-1]], axis=0)
        total += jnp.where(crow == wide - 1, 0.0, pltpu.roll(e, wide - 1, 1))
        total += jnp.where(crow == 0, 0.0, pltpu.roll(e, 1, 1))
        total += jnp.where(clane >= cz - COARSEN, 0.0, pltpu.roll(e, cz - COARSEN, 2))
        total += jnp.where(clane < COARSEN, 0.0, pltpu.roll(e, COARSEN, 2))
        return aj[...] + cj[...] * total

    e = lax.fori_loop(0, COARSE_ITERS - 1, jacobi, aj[...])
    ej[0] = zero_c[0]
    ej[n_span + 1] = zero_c[0]
    ej[1:n_span + 1] = e
    before, here, after = ej[s], ej[s + 1], ej[s + 2]

    def own_rows(v):
        out = v[:rows]
        for k in range(1, n_width):
            out = jnp.where(w == k, v[k * rows:(k + 1) * rows], out)
        return out

    y_low = jnp.zeros((1, cz), F32)
    y_high = jnp.zeros((1, cz), F32)
    for k in range(n_width):
        if k > 0:
            y_low = jnp.where(w == k, here[k * rows - 1:k * rows], y_low)
        if k < n_width - 1:
            y_high = jnp.where(w == k, here[(k + 1) * rows:(k + 1) * rows + 1], y_high)
    packed = jnp.concatenate(
        [own_rows(here), own_rows(before), own_rows(after), y_low, y_high,
         jnp.zeros((16 - 3 * rows - 2, cz), F32)], axis=0)
    for i in range(ions):
        v = jnp.where(eighth[:16] == i, packed, 0.0)
        if i:
            v = pltpu.roll(v, cz - i, 1)
        for step in (1, 2, 4):
            v = v + pltpu.roll(v, step, 1)
        sp[i] = v

    def tall(v):
        return jnp.concatenate(
            [jnp.broadcast_to(v[j:j + 1], (COARSEN, cz)) for j in range(rows)], axis=0)

    sums = []
    for i in range(ions):
        v = sp[i]
        lift = tall(v[:rows])
        lo, hi = tall(v[rows:2 * rows]), tall(v[2 * rows:3 * rows])
        base = yz_sum(lift) + lift
        base += jnp.where(first_y, v[3 * rows:3 * rows + 1], 0.0)
        base += jnp.where(last_y, v[3 * rows + 1:3 * rows + 2], 0.0)
        numer = jnp.zeros((cy, cz), F32)
        denom = jnp.zeros((cy, cz), F32)
        for h in range(2):
            for k in range(kp):
                side = lift
                low_side = p if h else jnp.logical_not(p)
                high_side = jnp.logical_not(p) if h else p
                if k == 0:
                    side = jnp.where(low_side, lo, side)
                if k == kp - 1:
                    side = jnp.where(high_side, hi, side)
                im = diag[h, i, k] * lift - spread_ref[i] * condp[h, k] * (base + side)
                image[h, i, k] = im
                numer += rhs[h, i, k] * im
                denom += im * im
        sums.append((jnp.sum(numer, axis=0, keepdims=True), jnp.sum(denom, axis=0, keepdims=True)))
    second[w] = jnp.concatenate([n for n, _ in sums] + [m for _, m in sums], axis=0)
    to_row(second, psend.at[0], precv.at[0])
    all_of(second, precv.at[0], n_width)
    part[s] = jnp.sum(second[...], axis=0)
    to_column(part, psend.at[1], precv.at[1])
    all_of(part, precv.at[1], n_span)
    whole = jnp.sum(jnp.sum(part[...], axis=0), axis=1, keepdims=True)
    weight = whole[:ions] / (whole[ions:] + EPSILON)
    wv[...] = jnp.broadcast_to(weight, (ions, cz))

    for i in range(ions):
        wt = wv[i:i + 1]
        lifted = wt * tall(sp[i, :rows])
        for k in range(kp):
            red, black = d[0, i, k], d[1, i, k]
            up_ref[i, 2 * k] = state_ref[i, 2 * k] + (jnp.where(p, black, red) + lifted)
            up_ref[i, 2 * k + 1] = state_ref[i, 2 * k + 1] + (jnp.where(p, red, black) + lifted)
            red = rhs[0, i, k] - wt * image[0, i, k]
            black = rhs[1, i, k] - wt * image[1, i, k]
            res_ref[i, 2 * k] = jnp.where(p, black, red)
            res_ref[i, 2 * k + 1] = jnp.where(p, red, black)

    for e in range(3):
        for k in range(4):
            @pl.when(has[k])
            def _():
                copy(e, k).wait_send()
    all_of(first, gsend.at[0], n_width)
    all_of(gath, gsend.at[1], n_span)
    all_of(second, psend.at[0], n_width)
    all_of(part, psend.at[1], n_span)


def on_device(n_span, n_width, state, source, conductance, rebar_cover, colour, diffusivity, binding):
    ions, cx, cy, cz = state.shape
    kp = cx // 2
    rows = cy // COARSEN
    half = pltpu.VMEM((2, ions, kp, cy, cz), F32)
    pair = pltpu.VMEM((2, kp, cy, cz), F32)
    vmem = pl.BlockSpec(memory_space=pltpu.VMEM)
    smem = pl.BlockSpec(memory_space=pltpu.SMEM)
    dma = pltpu.SemaphoreType.DMA
    return pl.pallas_call(
        functools.partial(kernel, n_span, n_width, ions, cx, cy, cz),
        out_shape=(jax.ShapeDtypeStruct(state.shape, F32),) * 2,
        in_specs=[pl.BlockSpec(memory_space=pltpu.HBM)] * 4 + [smem] * 3,
        out_specs=(vmem, vmem),
        scratch_shapes=[
            pltpu.VMEM(state.shape, F32), pltpu.VMEM(state.shape, F32),
            pltpu.VMEM(conductance.shape, F32), pltpu.VMEM(conductance.shape, jnp.int32),
            pltpu.VMEM((2, 2, ions, cy, cz), F32),
            pltpu.VMEM((3, 2, ions, cy, cz), F32),
            pltpu.VMEM((3, 2, ions, 2 * kp, cz), F32),
            pltpu.VMEM((3, 2, ions, 2 * kp, cz), F32),
            pltpu.VMEM((n_width, 2 * rows, cz), F32),
            pltpu.VMEM((n_span, n_width, 2 * rows, cz), F32),
            pltpu.VMEM((n_width, 2 * ions, cz), F32),
            pltpu.VMEM((n_span, 2 * ions, cz), F32),
            pair, pair, half, half, half, half, half, half,
            pltpu.VMEM((ions, cy, cz), F32),
            pltpu.VMEM((ions, cy, cz), F32),
            pltpu.VMEM((cy, cz), F32),
            pltpu.VMEM((n_span, n_width * rows, cz), F32),
            pltpu.VMEM((n_span, n_width * rows, cz), F32),
            pltpu.VMEM((n_span + 2, n_width * rows, cz), F32),
            pltpu.VMEM((ions, 16, cz), F32),
            pltpu.VMEM((ions, cz), F32),
            dma((3, 4)), dma((3, 4)), dma((2,)), dma((2,)), dma((2,)), dma((2,)), dma((4,)), pltpu.SemaphoreType.REGULAR((max(5, (n_span - 1).bit_length() + (n_width - 1).bit_length()),)),
        ],
        compiler_params=pltpu.CompilerParams(
            collective_id=0, has_side_effects=True, vmem_limit_bytes=60 * 1024 * 1024
        ),
    )(state, source, conductance, rebar_cover, colour, diffusivity, binding)


def solution(mesh):
    in_specs = (
        P(None, "span", "width", None),
        P(None, "span", "width", None),
        P("span", "width", None),
        P("span", "width", None),
        P("span", "width"),
        P(),
        P(),
    )
    out_specs = (P(None, "span", "width", None), P(None, "span", "width", None))
    return jax.shard_map(
        functools.partial(on_device, mesh.shape["span"], mesh.shape["width"]),
        mesh=mesh, in_specs=in_specs, out_specs=out_specs, check_vma=False,
    )
```

```python
import functools

import jax
import jax.numpy as jnp
from jax import lax
from jax.experimental import pallas as pl
from jax.experimental.pallas import tpu as pltpu
from jax.sharding import PartitionSpec as P

COARSEN = 8
SWEEPS = 4
COARSE_ITERS = 20
INV_STEP = 0.05
EPSILON = 1e-06
MESH = pl.DeviceIdType.MESH
F32 = jnp.float32


def kernel(
    n_span, n_width, ions, cx, cy, cz,
    state_hbm, source_hbm, cond_hbm, cover_hbm, colour_ref, spread_ref, strength_ref,
    up_ref, res_ref,
    state_ref, source_ref, cond_ref, cover_ref, xs, xh, ys, yh, first, gath, second, part, condp, coverp, rhs, diag, c, a, d, image,
    mx, fx, cx_sum, aj, cj, ej, sp, wv,
    send_sem, recv_sem, gsend, grecv, psend, precv, in_sem, met,
):
    s = lax.axis_index("span")
    w = lax.axis_index("width")
    kp = cx // 2
    rows = cy // COARSEN
    row = lax.broadcasted_iota(jnp.int32, (cy, cz), 0)
    lane = lax.broadcasted_iota(jnp.int32, (cy, cz), 1)
    p = (row + lane) % 2 == 1
    first_y, last_y = row == 0, row == cy - 1
    first_z, last_z = lane == 0, lane == cz - 1

    loads = [
        pltpu.make_async_copy(src, dst, in_sem.at[k])
        for k, (src, dst) in enumerate((
            (state_hbm, state_ref), (cond_hbm, cond_ref),
            (cover_hbm, cover_ref), (source_hbm, source_ref)))
    ]
    for load in loads:
        load.start()

    barrier = pltpu.get_barrier_semaphore()

    has = (s < n_span - 1, s > 0, w < n_width - 1, w > 0)
    gets = (s > 0, s < n_span - 1, w > 0, w < n_width - 1)
    to = ((s + 1, w), (s - 1, w), (s, w + 1), (s, w - 1))

    def flip(v, bit):
        return v + bit - 2 * bit * (v // bit % 2)

    bits = [1 << k for k in range((max(n_span, n_width) - 1).bit_length())]
    hops = [(s, flip(w, b)) for b in bits if b < n_width]
    hops += [(flip(s, b), w) for b in bits if b < n_span]
    far = [(s, flip(w, b)) for b in bits if 1 < b < n_width]
    far += [(flip(s, b), w) for b in bits if 1 < b < n_span]
    for k in range(4):
        @pl.when(has[k])
        def _():
            pl.semaphore_signal(barrier, inc=1, device_id=to[k], device_id_type=MESH)
    for other in far:
        pl.semaphore_signal(barrier, inc=1, device_id=other, device_id_type=MESH)

    def meet(which):
        for k in which:
            if 0 <= k < len(hops):
                pl.semaphore_signal(
                    met.at[k], inc=1, device_id=hops[k], device_id_type=MESH)

    def met_by(which):
        for k in which:
            if 0 <= k < len(hops):
                pl.semaphore_wait(met.at[k], 1)

    def split(x):
        pairs = x.reshape(kp, 2, cy, cz)
        even, odd = pairs[:, 0], pairs[:, 1]
        return jnp.where(p, odd, even), jnp.where(p, even, odd)

    def yz_sum(v):
        out = jnp.where(last_y, 0.0, pltpu.roll(v, cy - 1, v.ndim - 2))
        out += jnp.where(first_y, 0.0, pltpu.roll(v, 1, v.ndim - 2))
        out += jnp.where(last_z, 0.0, pltpu.roll(v, cz - 1, v.ndim - 1))
        out += jnp.where(first_z, 0.0, pltpu.roll(v, 1, v.ndim - 1))
        return out

    zero_face = jnp.zeros((1, cy, cz), F32)

    def nb_red(black):
        above = jnp.concatenate([black[1:], zero_face], axis=0)
        below = jnp.concatenate([zero_face, black[:-1]], axis=0)
        return black + jnp.where(p, above, below) + yz_sum(black)

    def nb_black(red):
        above = jnp.concatenate([red[1:], zero_face], axis=0)
        below = jnp.concatenate([zero_face, red[:-1]], axis=0)
        return red + jnp.where(p, below, above) + yz_sum(red)

    def rim(e, i):
        lo, hi = xh[e, 0, i], xh[e, 1, i]
        ylo, yhi = yh[e, 0, i], yh[e, 1, i]
        mid = jnp.zeros((kp - 2, cy, cz), F32)

        def faces(k0, k1, half):
            x_part = jnp.concatenate([k0[None], mid, k1[None]], axis=0)
            low = ylo[half * kp:(half + 1) * kp][:, None, :]
            high = yhi[half * kp:(half + 1) * kp][:, None, :]
            return x_part + jnp.where(first_y, low, 0.0) + jnp.where(last_y, high, 0.0)

        red = faces(jnp.where(p, 0.0, lo), jnp.where(p, hi, 0.0), 1)
        black = faces(jnp.where(p, lo, 0.0), jnp.where(p, 0.0, hi), 0)
        return red, black

    def put_y(e, i, red, black):
        ys[e, 0, i] = jnp.concatenate([red[:, cy - 1, :], black[:, cy - 1, :]], axis=0)
        ys[e, 1, i] = jnp.concatenate([red[:, 0, :], black[:, 0, :]], axis=0)

    def put_x(e, i, red, black):
        xs[e - 1, 0, i] = jnp.where(p, red[kp - 1], black[kp - 1])
        xs[e - 1, 1, i] = jnp.where(p, black[0], red[0])

    pair_of = ions // 2

    def copy(e, k, g):
        own = pl.ds(g * pair_of, pair_of)
        if k >= 2:
            src, dst = ys.at[e, k - 2, own], yh.at[e, k - 2, own]
        else:
            dst = xh.at[e, k, own]
            if e == 0:
                src = state_ref.at[own, cx - 1] if k == 0 else state_ref.at[own, 0]
            else:
                src = xs.at[e - 1, k, own]
        return pltpu.make_async_remote_copy(
            src_ref=src, dst_ref=dst, send_sem=send_sem.at[e, k, g], recv_sem=recv_sem.at[e, k, g],
            device_id=to[k], device_id_type=MESH,
        )

    def send(e, g):
        for k in range(4):
            @pl.when(has[k])
            def _():
                copy(e, k, g).start()

    def receive(e, g):
        for k in range(4):
            @pl.when(gets[k])
            def _():
                copy(e, k, g).wait_recv()

    for k in range(4):
        @pl.when(jnp.logical_not(gets[k]))
        def _():
            for e in range(3):
                if k >= 2:
                    yh[e, k - 2] = jnp.zeros(yh.shape[2:], F32)
                else:
                    xh[e, k] = jnp.zeros(xh.shape[2:], F32)

    def pack_state(i, _):
        put_y(0, i, *split(state_ref[i]))
        return 0

    loads[0].wait()
    lax.fori_loop(0, ions, pack_state, 0)
    near = sum(g.astype(jnp.int32) for g in gets)
    pl.semaphore_wait(barrier, near + len(far))
    send(0, 0)
    send(0, 1)
    meet((0,))

    for load in loads[1:]:
        load.wait()
    condp[0], condp[1] = split(cond_ref[...])
    coverp[0], coverp[1] = split(cover_ref[...].astype(F32))
    cx_sum[...] = jnp.sum(cond_ref[...], axis=0)

    def local_terms(i, _):
        spread, strength = spread_ref[i], strength_ref[i]
        st = split(state_ref[i])
        src = split(source_ref[i])
        near = (nb_red(st[1]), nb_black(st[0]))
        mass_sum = jnp.zeros((cy, cz), F32)
        for h in range(2):
            coef = spread * condp[h]
            inv = 1.0 / (1.0 + st[h])
            bound = coverp[h] * strength * inv
            mass = INV_STEP + bound * inv
            dg = mass + 6.0 * coef
            diag[h, i] = dg
            c[h, i] = coef / dg
            rhs[h, i] = src[h] - (coef * (6.0 * st[h] - near[h]) + bound * st[h])
            mass_sum += jnp.sum(mass, axis=0)
        mx[i] = mass_sum
        return 0

    lax.fori_loop(0, ions, local_terms, 0)
    met_by((0,))
    meet((1,))

    mine = colour_ref[0, 0].astype(F32)

    def sweeps(ar, ab, cr, cb):
        red = ar
        black = ab + cb * nb_black(red)
        for _ in range(SWEEPS - 1):
            red = ar + cr * nb_red(black)
            black = ab + cb * nb_black(red)
        return red, black

    def phase_zero(i, _):
        near = rim(0, i)
        for h in range(2):
            right = rhs[h, i] + spread_ref[i] * condp[h] * near[h]
            rhs[h, i] = right
            a[h, i] = right / diag[h, i]
        red, black = sweeps(
            (1.0 - mine) * a[0, i], (1.0 - mine) * a[1, i], c[0, i], c[1, i]
        )
        d[0, i], d[1, i] = red, black
        put_y(1, i, red, black)
        put_x(1, i, red, black)
        return 0

    def halves(e, body):
        for g in range(2):
            receive(e, g)
            lax.fori_loop(g * pair_of, (g + 1) * pair_of, body, 0, unroll=2)
            if e < 2:
                send(e + 1, g)

    halves(0, phase_zero)
    met_by((1,))
    meet((2,))
    met_by((2,))
    meet((3,))

    def phase_one(i, _):
        near = rim(1, i)
        red, black = sweeps(
            mine * (a[0, i] + c[0, i] * near[0]), mine * (a[1, i] + c[1, i] * near[1]),
            c[0, i], c[1, i],
        )
        red, black = red + d[0, i], black + d[1, i]
        d[0, i], d[1, i] = red, black
        put_y(2, i, red, black)
        put_x(2, i, red, black)
        return 0

    halves(1, phase_one)
    met_by((3,))
    meet((4,))

    eighth = lane % COARSEN

    def coarse_pack(parts):
        acc = jnp.zeros((cy, cz), F32)
        for i in range(ions):
            v = parts[i]
            for step in (1, 2, 4):
                v = v + pltpu.roll(v, cz - step, 1)
            if i:
                v = pltpu.roll(v, i, 1)
            acc = jnp.where(eighth == i, v, acc)
        return jnp.concatenate(
            [jnp.sum(acc[j * COARSEN:(j + 1) * COARSEN], axis=0, keepdims=True)
             for j in range(rows)], axis=0)

    cond_sum = cx_sum[...]
    coarse_off = coarse_pack([spread_ref[i] * cond_sum for i in range(ions)]) / COARSEN
    coarse_diag = coarse_pack([mx[i] for i in range(ions)]) + 6.0 * coarse_off
    coarse_inv = 1.0 / jnp.where(eighth[:rows] < ions, coarse_diag, 1.0)


    def fine_terms(i, _):
        near = rim(2, i)
        red, black = d[0, i], d[1, i]
        near = (near[0] + nb_red(black), near[1] + nb_black(red))
        total = jnp.zeros((cy, cz), F32)
        for h, v in ((0, red), (1, black)):
            fine = rhs[h, i] - (diag[h, i] * v - spread_ref[i] * condp[h] * near[h])
            rhs[h, i] = fine
            total += jnp.sum(fine, axis=0)
        fx[i] = total
        return 0

    met_by((4,))
    for k in range(5, len(hops)):
        meet((k,))
        met_by((k,))
    halves(2, fine_terms)
    crhs = coarse_pack([fx[i] for i in range(ions)])
    first[w] = jnp.concatenate([crhs * coarse_inv, coarse_off * coarse_inv], axis=0)

    def to_row(buf, ssem, rsem):
        for off in range(1, n_width):
            pltpu.make_async_remote_copy(
                src_ref=buf.at[w], dst_ref=buf.at[w], send_sem=ssem, recv_sem=rsem,
                device_id=(s, lax.rem(w + off, n_width)), device_id_type=MESH,
            ).start()

    def to_column(buf, ssem, rsem):
        @pl.loop(1, n_span)
        def _(off):
            pltpu.make_async_remote_copy(
                src_ref=buf.at[s], dst_ref=buf.at[s], send_sem=ssem, recv_sem=rsem,
                device_id=(lax.rem(s + off, n_span), w), device_id_type=MESH,
            ).start()

    def all_of(buf, sem, count):
        others = buf.at[pl.ds(0, count - 1)]
        pltpu.make_async_copy(others, others, sem).wait()

    to_row(first, gsend.at[0], grecv.at[0])
    all_of(first, grecv.at[0], n_width)
    gath[s] = first[...]
    to_column(gath, gsend.at[1], grecv.at[1])
    all_of(gath, grecv.at[1], n_span)

    wide = n_width * rows
    g = gath[...]
    aj[...] = jnp.concatenate([g[:, k, :rows] for k in range(n_width)], axis=1)
    cj[...] = jnp.concatenate([g[:, k, rows:] for k in range(n_width)], axis=1)
    crow = lax.broadcasted_iota(jnp.int32, (wide, cz), 0)
    clane = lax.broadcasted_iota(jnp.int32, (wide, cz), 1)
    zero_c = jnp.zeros((1, wide, cz), F32)

    def jacobi(_, e):
        total = jnp.concatenate([e[1:], zero_c], axis=0)
        total += jnp.concatenate([zero_c, e[:-1]], axis=0)
        total += jnp.where(crow == wide - 1, 0.0, pltpu.roll(e, wide - 1, 1))
        total += jnp.where(crow == 0, 0.0, pltpu.roll(e, 1, 1))
        total += jnp.where(clane >= cz - COARSEN, 0.0, pltpu.roll(e, cz - COARSEN, 2))
        total += jnp.where(clane < COARSEN, 0.0, pltpu.roll(e, COARSEN, 2))
        return aj[...] + cj[...] * total

    e = lax.fori_loop(0, COARSE_ITERS - 1, jacobi, aj[...])
    ej[0] = zero_c[0]
    ej[n_span + 1] = zero_c[0]
    ej[1:n_span + 1] = e
    before, here, after = ej[s], ej[s + 1], ej[s + 2]

    def own_rows(v):
        out = v[:rows]
        for k in range(1, n_width):
            out = jnp.where(w == k, v[k * rows:(k + 1) * rows], out)
        return out

    y_low = jnp.zeros((1, cz), F32)
    y_high = jnp.zeros((1, cz), F32)
    for k in range(n_width):
        if k > 0:
            y_low = jnp.where(w == k, here[k * rows - 1:k * rows], y_low)
        if k < n_width - 1:
            y_high = jnp.where(w == k, here[(k + 1) * rows:(k + 1) * rows + 1], y_high)
    packed = jnp.concatenate(
        [own_rows(here), own_rows(before), own_rows(after), y_low, y_high,
         jnp.zeros((16 - 3 * rows - 2, cz), F32)], axis=0)
    for i in range(ions):
        v = jnp.where(eighth[:16] == i, packed, 0.0)
        if i:
            v = pltpu.roll(v, cz - i, 1)
        for step in (1, 2, 4):
            v = v + pltpu.roll(v, step, 1)
        sp[i] = v

    def tall(v):
        return jnp.concatenate(
            [jnp.broadcast_to(v[j:j + 1], (COARSEN, cz)) for j in range(rows)], axis=0)

    sums = []
    for i in range(ions):
        v = sp[i]
        lift = tall(v[:rows])
        lo, hi = tall(v[rows:2 * rows]), tall(v[2 * rows:3 * rows])
        base = yz_sum(lift) + lift
        base += jnp.where(first_y, v[3 * rows:3 * rows + 1], 0.0)
        base += jnp.where(last_y, v[3 * rows + 1:3 * rows + 2], 0.0)
        numer = jnp.zeros((cy, cz), F32)
        denom = jnp.zeros((cy, cz), F32)
        for h in range(2):
            for k in range(kp):
                side = lift
                low_side = p if h else jnp.logical_not(p)
                high_side = jnp.logical_not(p) if h else p
                if k == 0:
                    side = jnp.where(low_side, lo, side)
                if k == kp - 1:
                    side = jnp.where(high_side, hi, side)
                im = diag[h, i, k] * lift - spread_ref[i] * condp[h, k] * (base + side)
                image[h, i, k] = im
                numer += rhs[h, i, k] * im
                denom += im * im
        sums.append((jnp.sum(numer, axis=0, keepdims=True), jnp.sum(denom, axis=0, keepdims=True)))
    second[w] = jnp.concatenate([n for n, _ in sums] + [m for _, m in sums], axis=0)
    to_row(second, psend.at[0], precv.at[0])
    all_of(second, precv.at[0], n_width)
    part[s] = jnp.sum(second[...], axis=0)
    to_column(part, psend.at[1], precv.at[1])
    all_of(part, precv.at[1], n_span)
    whole = jnp.sum(jnp.sum(part[...], axis=0), axis=1, keepdims=True)
    weight = whole[:ions] / (whole[ions:] + EPSILON)
    wv[...] = jnp.broadcast_to(weight, (ions, cz))

    for i in range(ions):
        wt = wv[i:i + 1]
        lifted = wt * tall(sp[i, :rows])
        for k in range(kp):
            red, black = d[0, i, k], d[1, i, k]
            up_ref[i, 2 * k] = state_ref[i, 2 * k] + (jnp.where(p, black, red) + lifted)
            up_ref[i, 2 * k + 1] = state_ref[i, 2 * k + 1] + (jnp.where(p, red, black) + lifted)
            red = rhs[0, i, k] - wt * image[0, i, k]
            black = rhs[1, i, k] - wt * image[1, i, k]
            res_ref[i, 2 * k] = jnp.where(p, black, red)
            res_ref[i, 2 * k + 1] = jnp.where(p, red, black)

    for e in range(3):
        for k in range(4):
            @pl.when(has[k])
            def _():
                copy(e, k, 0).wait_send()
                copy(e, k, 1).wait_send()
    all_of(first, gsend.at[0], n_width)
    all_of(gath, gsend.at[1], n_span)
    all_of(second, psend.at[0], n_width)
    all_of(part, psend.at[1], n_span)


def on_device(n_span, n_width, state, source, conductance, rebar_cover, colour, diffusivity, binding):
    ions, cx, cy, cz = state.shape
    kp = cx // 2
    rows = cy // COARSEN
    half = pltpu.VMEM((2, ions, kp, cy, cz), F32)
    pair = pltpu.VMEM((2, kp, cy, cz), F32)
    vmem = pl.BlockSpec(memory_space=pltpu.VMEM)
    smem = pl.BlockSpec(memory_space=pltpu.SMEM)
    dma = pltpu.SemaphoreType.DMA
    return pl.pallas_call(
        functools.partial(kernel, n_span, n_width, ions, cx, cy, cz),
        out_shape=(jax.ShapeDtypeStruct(state.shape, F32),) * 2,
        in_specs=[pl.BlockSpec(memory_space=pltpu.HBM)] * 4 + [smem] * 3,
        out_specs=(vmem, vmem),
        scratch_shapes=[
            pltpu.VMEM(state.shape, F32), pltpu.VMEM(state.shape, F32),
            pltpu.VMEM(conductance.shape, F32), pltpu.VMEM(conductance.shape, jnp.int32),
            pltpu.VMEM((2, 2, ions, cy, cz), F32),
            pltpu.VMEM((3, 2, ions, cy, cz), F32),
            pltpu.VMEM((3, 2, ions, 2 * kp, cz), F32),
            pltpu.VMEM((3, 2, ions, 2 * kp, cz), F32),
            pltpu.VMEM((n_width, 2 * rows, cz), F32),
            pltpu.VMEM((n_span, n_width, 2 * rows, cz), F32),
            pltpu.VMEM((n_width, 2 * ions, cz), F32),
            pltpu.VMEM((n_span, 2 * ions, cz), F32),
            pair, pair, half, half, half, half, half, half,
            pltpu.VMEM((ions, cy, cz), F32),
            pltpu.VMEM((ions, cy, cz), F32),
            pltpu.VMEM((cy, cz), F32),
            pltpu.VMEM((n_span, n_width * rows, cz), F32),
            pltpu.VMEM((n_span, n_width * rows, cz), F32),
            pltpu.VMEM((n_span + 2, n_width * rows, cz), F32),
            pltpu.VMEM((ions, 16, cz), F32),
            pltpu.VMEM((ions, cz), F32),
            dma((3, 4, 2)), dma((3, 4, 2)), dma((2,)), dma((2,)), dma((2,)), dma((2,)), dma((4,)), pltpu.SemaphoreType.REGULAR((max(5, (n_span - 1).bit_length() + (n_width - 1).bit_length()),)),
        ],
        compiler_params=pltpu.CompilerParams(
            collective_id=0, has_side_effects=True, vmem_limit_bytes=60 * 1024 * 1024
        ),
    )(state, source, conductance, rebar_cover, colour, diffusivity, binding)


def solution(mesh):
    in_specs = (
        P(None, "span", "width", None),
        P(None, "span", "width", None),
        P("span", "width", None),
        P("span", "width", None),
        P("span", "width"),
        P(),
        P(),
    )
    out_specs = (P(None, "span", "width", None), P(None, "span", "width", None))
    return jax.shard_map(
        functools.partial(on_device, mesh.shape["span"], mesh.shape["width"]),
        mesh=mesh, in_specs=in_specs, out_specs=out_specs, check_vma=False,
    )
```

```python
import functools

import jax
import jax.numpy as jnp
from jax import lax
from jax.experimental import pallas as pl
from jax.experimental.pallas import tpu as pltpu
from jax.sharding import PartitionSpec as P

COARSEN = 8
SWEEPS = 4
COARSE_ITERS = 20
INV_STEP = 0.05
EPSILON = 1e-06
MESH = pl.DeviceIdType.MESH
F32 = jnp.float32


def kernel(
    n_span, n_width, ions, cx, cy, cz,
    state_hbm, source_hbm, cond_hbm, cover_hbm, colour_ref, spread_ref, strength_ref,
    up_ref, res_ref,
    state_ref, source_ref, cond_ref, cover_ref, xs, xh, ys, yh, first, gath, part, condp, coverp, rhs, diag, c, a, d, image,
    mx, fx, cx_sum, aj, cj, ej, sp, wv,
    send_sem, recv_sem, gsend, grecv, psend, precv, in_sem, met,
):
    s = lax.axis_index("span")
    w = lax.axis_index("width")
    kp = cx // 2
    rows = cy // COARSEN
    row = lax.broadcasted_iota(jnp.int32, (cy, cz), 0)
    lane = lax.broadcasted_iota(jnp.int32, (cy, cz), 1)
    p = (row + lane) % 2 == 1
    first_y, last_y = row == 0, row == cy - 1
    first_z, last_z = lane == 0, lane == cz - 1

    loads = [
        pltpu.make_async_copy(src, dst, in_sem.at[k])
        for k, (src, dst) in enumerate((
            (state_hbm, state_ref), (cond_hbm, cond_ref),
            (cover_hbm, cover_ref), (source_hbm, source_ref)))
    ]
    for load in loads:
        load.start()

    barrier = pltpu.get_barrier_semaphore()

    has = (s < n_span - 1, s > 0, w < n_width - 1, w > 0)
    gets = (s > 0, s < n_span - 1, w > 0, w < n_width - 1)
    to = ((s + 1, w), (s - 1, w), (s, w + 1), (s, w - 1))

    def flip(v, bit):
        return v + bit - 2 * bit * (v // bit % 2)

    bits = [1 << k for k in range((max(n_span, n_width) - 1).bit_length())]
    hops = [(s, flip(w, b)) for b in bits if b < n_width]
    hops += [(flip(s, b), w) for b in bits if b < n_span]
    far = [(s, flip(w, b)) for b in bits if 1 < b < n_width]
    far += [(flip(s, b), w) for b in bits if 1 < b < n_span]
    for k in range(4):
        @pl.when(has[k])
        def _():
            pl.semaphore_signal(barrier, inc=1, device_id=to[k], device_id_type=MESH)
    for other in far:
        pl.semaphore_signal(barrier, inc=1, device_id=other, device_id_type=MESH)

    def meet(which):
        for k in which:
            if 0 <= k < len(hops):
                pl.semaphore_signal(
                    met.at[k], inc=1, device_id=hops[k], device_id_type=MESH)

    def met_by(which):
        for k in which:
            if 0 <= k < len(hops):
                pl.semaphore_wait(met.at[k], 1)

    def split(x):
        pairs = x.reshape(kp, 2, cy, cz)
        even, odd = pairs[:, 0], pairs[:, 1]
        return jnp.where(p, odd, even), jnp.where(p, even, odd)

    def yz_sum(v):
        out = jnp.where(last_y, 0.0, pltpu.roll(v, cy - 1, v.ndim - 2))
        out += jnp.where(first_y, 0.0, pltpu.roll(v, 1, v.ndim - 2))
        out += jnp.where(last_z, 0.0, pltpu.roll(v, cz - 1, v.ndim - 1))
        out += jnp.where(first_z, 0.0, pltpu.roll(v, 1, v.ndim - 1))
        return out

    zero_face = jnp.zeros((1, cy, cz), F32)

    def nb_red(black):
        above = jnp.concatenate([black[1:], zero_face], axis=0)
        below = jnp.concatenate([zero_face, black[:-1]], axis=0)
        return black + jnp.where(p, above, below) + yz_sum(black)

    def nb_black(red):
        above = jnp.concatenate([red[1:], zero_face], axis=0)
        below = jnp.concatenate([zero_face, red[:-1]], axis=0)
        return red + jnp.where(p, below, above) + yz_sum(red)

    def rim(e, i):
        lo, hi = xh[e, 0, i], xh[e, 1, i]
        ylo, yhi = yh[e, 0, i], yh[e, 1, i]
        mid = jnp.zeros((kp - 2, cy, cz), F32)

        def faces(k0, k1, half):
            x_part = jnp.concatenate([k0[None], mid, k1[None]], axis=0)
            low = ylo[half * kp:(half + 1) * kp][:, None, :]
            high = yhi[half * kp:(half + 1) * kp][:, None, :]
            return x_part + jnp.where(first_y, low, 0.0) + jnp.where(last_y, high, 0.0)

        red = faces(jnp.where(p, 0.0, lo), jnp.where(p, hi, 0.0), 1)
        black = faces(jnp.where(p, lo, 0.0), jnp.where(p, 0.0, hi), 0)
        return red, black

    def put_y(e, i, red, black):
        ys[e, 0, i] = jnp.concatenate([red[:, cy - 1, :], black[:, cy - 1, :]], axis=0)
        ys[e, 1, i] = jnp.concatenate([red[:, 0, :], black[:, 0, :]], axis=0)

    def put_x(e, i, red, black):
        xs[e - 1, 0, i] = jnp.where(p, red[kp - 1], black[kp - 1])
        xs[e - 1, 1, i] = jnp.where(p, black[0], red[0])

    pair_of = ions // 2

    def copy(e, k, g):
        own = pl.ds(g * pair_of, pair_of)
        if k >= 2:
            src, dst = ys.at[e, k - 2, own], yh.at[e, k - 2, own]
        else:
            dst = xh.at[e, k, own]
            if e == 0:
                src = state_ref.at[own, cx - 1] if k == 0 else state_ref.at[own, 0]
            else:
                src = xs.at[e - 1, k, own]
        return pltpu.make_async_remote_copy(
            src_ref=src, dst_ref=dst, send_sem=send_sem.at[e, k, g], recv_sem=recv_sem.at[e, k, g],
            device_id=to[k], device_id_type=MESH,
        )

    def send(e, g):
        for k in range(4):
            @pl.when(has[k])
            def _():
                copy(e, k, g).start()

    def receive(e, g):
        for k in range(4):
            @pl.when(gets[k])
            def _():
                copy(e, k, g).wait_recv()

    for k in range(4):
        @pl.when(jnp.logical_not(gets[k]))
        def _():
            for e in range(3):
                if k >= 2:
                    yh[e, k - 2] = jnp.zeros(yh.shape[2:], F32)
                else:
                    xh[e, k] = jnp.zeros(xh.shape[2:], F32)

    def pack_state(i, _):
        put_y(0, i, *split(state_ref[i]))
        return 0

    loads[0].wait()
    lax.fori_loop(0, ions, pack_state, 0)
    near = sum(g.astype(jnp.int32) for g in gets)
    pl.semaphore_wait(barrier, near + len(far))
    send(0, 0)
    send(0, 1)
    meet((0,))

    for load in loads[1:]:
        load.wait()
    condp[0], condp[1] = split(cond_ref[...])
    coverp[0], coverp[1] = split(cover_ref[...].astype(F32))
    cx_sum[...] = jnp.sum(cond_ref[...], axis=0)

    def local_terms(i, _):
        spread, strength = spread_ref[i], strength_ref[i]
        st = split(state_ref[i])
        src = split(source_ref[i])
        near = (nb_red(st[1]), nb_black(st[0]))
        mass_sum = jnp.zeros((cy, cz), F32)
        for h in range(2):
            coef = spread * condp[h]
            inv = 1.0 / (1.0 + st[h])
            bound = coverp[h] * strength * inv
            mass = INV_STEP + bound * inv
            dg = mass + 6.0 * coef
            diag[h, i] = dg
            c[h, i] = coef / dg
            rhs[h, i] = src[h] - (coef * (6.0 * st[h] - near[h]) + bound * st[h])
            mass_sum += jnp.sum(mass, axis=0)
        mx[i] = mass_sum
        return 0

    lax.fori_loop(0, ions, local_terms, 0)
    met_by((0,))
    meet((1,))

    mine = colour_ref[0, 0].astype(F32)

    def sweeps(ar, ab, cr, cb):
        red = ar
        black = ab + cb * nb_black(red)
        for _ in range(SWEEPS - 1):
            red = ar + cr * nb_red(black)
            black = ab + cb * nb_black(red)
        return red, black

    def phase_zero(i, _):
        near = rim(0, i)
        for h in range(2):
            right = rhs[h, i] + spread_ref[i] * condp[h] * near[h]
            rhs[h, i] = right
            a[h, i] = right / diag[h, i]
        red, black = sweeps(
            (1.0 - mine) * a[0, i], (1.0 - mine) * a[1, i], c[0, i], c[1, i]
        )
        d[0, i], d[1, i] = red, black
        put_y(1, i, red, black)
        put_x(1, i, red, black)
        return 0

    def halves(e, body):
        for g in range(2):
            receive(e, g)
            lax.fori_loop(g * pair_of, (g + 1) * pair_of, body, 0, unroll=2)
            if e < 2:
                send(e + 1, g)

    halves(0, phase_zero)
    met_by((1,))
    meet((2,))
    met_by((2,))
    meet((3,))

    def phase_one(i, _):
        near = rim(1, i)
        red, black = sweeps(
            mine * (a[0, i] + c[0, i] * near[0]), mine * (a[1, i] + c[1, i] * near[1]),
            c[0, i], c[1, i],
        )
        red, black = red + d[0, i], black + d[1, i]
        d[0, i], d[1, i] = red, black
        put_y(2, i, red, black)
        put_x(2, i, red, black)
        return 0

    halves(1, phase_one)
    met_by((3,))
    meet((4,))

    eighth = lane % COARSEN

    def coarse_pack(parts):
        acc = jnp.zeros((cy, cz), F32)
        for i in range(ions):
            v = parts[i]
            for step in (1, 2, 4):
                v = v + pltpu.roll(v, cz - step, 1)
            if i:
                v = pltpu.roll(v, i, 1)
            acc = jnp.where(eighth == i, v, acc)
        return jnp.concatenate(
            [jnp.sum(acc[j * COARSEN:(j + 1) * COARSEN], axis=0, keepdims=True)
             for j in range(rows)], axis=0)

    cond_sum = cx_sum[...]
    coarse_off = coarse_pack([spread_ref[i] * cond_sum for i in range(ions)]) / COARSEN
    coarse_diag = coarse_pack([mx[i] for i in range(ions)]) + 6.0 * coarse_off
    coarse_inv = 1.0 / jnp.where(eighth[:rows] < ions, coarse_diag, 1.0)


    def fine_terms(i, _):
        near = rim(2, i)
        red, black = d[0, i], d[1, i]
        near = (near[0] + nb_red(black), near[1] + nb_black(red))
        total = jnp.zeros((cy, cz), F32)
        for h, v in ((0, red), (1, black)):
            fine = rhs[h, i] - (diag[h, i] * v - spread_ref[i] * condp[h] * near[h])
            rhs[h, i] = fine
            total += jnp.sum(fine, axis=0)
        fx[i] = total
        return 0

    met_by((4,))
    for k in range(5, len(hops)):
        meet((k,))
        met_by((k,))
    halves(2, fine_terms)
    crhs = coarse_pack([fx[i] for i in range(ions)])
    first[w] = jnp.concatenate([crhs * coarse_inv, coarse_off * coarse_inv], axis=0)

    def to_row(buf, ssem, rsem):
        for off in range(1, n_width):
            pltpu.make_async_remote_copy(
                src_ref=buf.at[w], dst_ref=buf.at[w], send_sem=ssem, recv_sem=rsem,
                device_id=(s, lax.rem(w + off, n_width)), device_id_type=MESH,
            ).start()

    def to_column(buf, ssem, rsem):
        @pl.loop(1, n_span)
        def _(off):
            pltpu.make_async_remote_copy(
                src_ref=buf.at[s], dst_ref=buf.at[s], send_sem=ssem, recv_sem=rsem,
                device_id=(lax.rem(s + off, n_span), w), device_id_type=MESH,
            ).start()

    def all_of(buf, sem, count):
        others = buf.at[pl.ds(0, count - 1)]
        pltpu.make_async_copy(others, others, sem).wait()

    to_row(first, gsend.at[0], grecv.at[0])
    all_of(first, grecv.at[0], n_width)
    gath[s] = first[...]
    to_column(gath, gsend.at[1], grecv.at[1])
    all_of(gath, grecv.at[1], n_span)

    wide = n_width * rows
    g = gath[...]
    aj[...] = jnp.concatenate([g[:, k, :rows] for k in range(n_width)], axis=1)
    cj[...] = jnp.concatenate([g[:, k, rows:] for k in range(n_width)], axis=1)
    crow = lax.broadcasted_iota(jnp.int32, (wide, cz), 0)
    clane = lax.broadcasted_iota(jnp.int32, (wide, cz), 1)
    zero_c = jnp.zeros((1, wide, cz), F32)

    def jacobi(_, e):
        total = jnp.concatenate([e[1:], zero_c], axis=0)
        total += jnp.concatenate([zero_c, e[:-1]], axis=0)
        total += jnp.where(crow == wide - 1, 0.0, pltpu.roll(e, wide - 1, 1))
        total += jnp.where(crow == 0, 0.0, pltpu.roll(e, 1, 1))
        total += jnp.where(clane >= cz - COARSEN, 0.0, pltpu.roll(e, cz - COARSEN, 2))
        total += jnp.where(clane < COARSEN, 0.0, pltpu.roll(e, COARSEN, 2))
        return aj[...] + cj[...] * total

    e = lax.fori_loop(0, COARSE_ITERS - 1, jacobi, aj[...])
    ej[0] = zero_c[0]
    ej[n_span + 1] = zero_c[0]
    ej[1:n_span + 1] = e
    before, here, after = ej[s], ej[s + 1], ej[s + 2]

    def own_rows(v):
        out = v[:rows]
        for k in range(1, n_width):
            out = jnp.where(w == k, v[k * rows:(k + 1) * rows], out)
        return out

    y_low = jnp.zeros((1, cz), F32)
    y_high = jnp.zeros((1, cz), F32)
    for k in range(n_width):
        if k > 0:
            y_low = jnp.where(w == k, here[k * rows - 1:k * rows], y_low)
        if k < n_width - 1:
            y_high = jnp.where(w == k, here[(k + 1) * rows:(k + 1) * rows + 1], y_high)
    packed = jnp.concatenate(
        [own_rows(here), own_rows(before), own_rows(after), y_low, y_high,
         jnp.zeros((16 - 3 * rows - 2, cz), F32)], axis=0)
    for i in range(ions):
        v = jnp.where(eighth[:16] == i, packed, 0.0)
        if i:
            v = pltpu.roll(v, cz - i, 1)
        for step in (1, 2, 4):
            v = v + pltpu.roll(v, step, 1)
        sp[i] = v

    def tall(v):
        return jnp.concatenate(
            [jnp.broadcast_to(v[j:j + 1], (COARSEN, cz)) for j in range(rows)], axis=0)

    sums = []
    for i in range(ions):
        v = sp[i]
        lift = tall(v[:rows])
        lo, hi = tall(v[rows:2 * rows]), tall(v[2 * rows:3 * rows])
        base = yz_sum(lift) + lift
        base += jnp.where(first_y, v[3 * rows:3 * rows + 1], 0.0)
        base += jnp.where(last_y, v[3 * rows + 1:3 * rows + 2], 0.0)
        numer = jnp.zeros((cy, cz), F32)
        denom = jnp.zeros((cy, cz), F32)
        for h in range(2):
            for k in range(kp):
                side = lift
                low_side = p if h else jnp.logical_not(p)
                high_side = jnp.logical_not(p) if h else p
                if k == 0:
                    side = jnp.where(low_side, lo, side)
                if k == kp - 1:
                    side = jnp.where(high_side, hi, side)
                im = diag[h, i, k] * lift - spread_ref[i] * condp[h, k] * (base + side)
                image[h, i, k] = im
                numer += rhs[h, i, k] * im
                denom += im * im
        sums.append((jnp.sum(numer, axis=0, keepdims=True), jnp.sum(denom, axis=0, keepdims=True)))
    me = s * n_width + w
    part[me] = jnp.concatenate([n for n, _ in sums] + [m for _, m in sums], axis=0)
    everyone = n_span * n_width

    @pl.loop(1, everyone)
    def _(off):
        other = lax.rem(me + off, everyone)
        pltpu.make_async_remote_copy(
            src_ref=part.at[me], dst_ref=part.at[me], send_sem=psend, recv_sem=precv,
            device_id=(other // n_width, other % n_width), device_id_type=MESH,
        ).start()

    all_of(part, precv, everyone)
    whole = jnp.sum(jnp.sum(part[...], axis=0), axis=1, keepdims=True)
    weight = whole[:ions] / (whole[ions:] + EPSILON)
    wv[...] = jnp.broadcast_to(weight, (ions, cz))

    for i in range(ions):
        wt = wv[i:i + 1]
        lifted = wt * tall(sp[i, :rows])
        for k in range(kp):
            red, black = d[0, i, k], d[1, i, k]
            up_ref[i, 2 * k] = state_ref[i, 2 * k] + (jnp.where(p, black, red) + lifted)
            up_ref[i, 2 * k + 1] = state_ref[i, 2 * k + 1] + (jnp.where(p, red, black) + lifted)
            red = rhs[0, i, k] - wt * image[0, i, k]
            black = rhs[1, i, k] - wt * image[1, i, k]
            res_ref[i, 2 * k] = jnp.where(p, black, red)
            res_ref[i, 2 * k + 1] = jnp.where(p, red, black)

    for e in range(3):
        for k in range(4):
            @pl.when(has[k])
            def _():
                copy(e, k, 0).wait_send()
                copy(e, k, 1).wait_send()
    all_of(first, gsend.at[0], n_width)
    all_of(gath, gsend.at[1], n_span)
    all_of(part, psend, everyone)


def on_device(n_span, n_width, state, source, conductance, rebar_cover, colour, diffusivity, binding):
    ions, cx, cy, cz = state.shape
    kp = cx // 2
    rows = cy // COARSEN
    half = pltpu.VMEM((2, ions, kp, cy, cz), F32)
    pair = pltpu.VMEM((2, kp, cy, cz), F32)
    vmem = pl.BlockSpec(memory_space=pltpu.VMEM)
    smem = pl.BlockSpec(memory_space=pltpu.SMEM)
    dma = pltpu.SemaphoreType.DMA
    return pl.pallas_call(
        functools.partial(kernel, n_span, n_width, ions, cx, cy, cz),
        out_shape=(jax.ShapeDtypeStruct(state.shape, F32),) * 2,
        in_specs=[pl.BlockSpec(memory_space=pltpu.HBM)] * 4 + [smem] * 3,
        out_specs=(vmem, vmem),
        scratch_shapes=[
            pltpu.VMEM(state.shape, F32), pltpu.VMEM(state.shape, F32),
            pltpu.VMEM(conductance.shape, F32), pltpu.VMEM(conductance.shape, jnp.int32),
            pltpu.VMEM((2, 2, ions, cy, cz), F32),
            pltpu.VMEM((3, 2, ions, cy, cz), F32),
            pltpu.VMEM((3, 2, ions, 2 * kp, cz), F32),
            pltpu.VMEM((3, 2, ions, 2 * kp, cz), F32),
            pltpu.VMEM((n_width, 2 * rows, cz), F32),
            pltpu.VMEM((n_span, n_width, 2 * rows, cz), F32),
            pltpu.VMEM((n_span * n_width, 2 * ions, cz), F32),
            pair, pair, half, half, half, half, half, half,
            pltpu.VMEM((ions, cy, cz), F32),
            pltpu.VMEM((ions, cy, cz), F32),
            pltpu.VMEM((cy, cz), F32),
            pltpu.VMEM((n_span, n_width * rows, cz), F32),
            pltpu.VMEM((n_span, n_width * rows, cz), F32),
            pltpu.VMEM((n_span + 2, n_width * rows, cz), F32),
            pltpu.VMEM((ions, 16, cz), F32),
            pltpu.VMEM((ions, cz), F32),
            dma((3, 4, 2)), dma((3, 4, 2)), dma((2,)), dma((2,)), dma, dma, dma((4,)), pltpu.SemaphoreType.REGULAR((max(5, (n_span - 1).bit_length() + (n_width - 1).bit_length()),)),
        ],
        compiler_params=pltpu.CompilerParams(
            collective_id=0, has_side_effects=True, vmem_limit_bytes=60 * 1024 * 1024
        ),
    )(state, source, conductance, rebar_cover, colour, diffusivity, binding)


def solution(mesh):
    in_specs = (
        P(None, "span", "width", None),
        P(None, "span", "width", None),
        P("span", "width", None),
        P("span", "width", None),
        P("span", "width"),
        P(),
        P(),
    )
    out_specs = (P(None, "span", "width", None), P(None, "span", "width", None))
    return jax.shard_map(
        functools.partial(on_device, mesh.shape["span"], mesh.shape["width"]),
        mesh=mesh, in_specs=in_specs, out_specs=out_specs, check_vma=False,
    )
```
